512 devices in a mesh: island: 4 (over z_hi), section: 16 (over y, z_lo), fsdp: 8 (over x, core).
Axes of the slice: x: 4, y: 8, z: 8 (z_hi: 4, z_lo: 2; z = z_hi * 2 + z_lo), core: 2. Of those that a mesh axis runs over, the one named last changes fastest.
Arguments:
- hidden: bfloat16 [4, 16, 1024, 4096], P('island', 'section', 'fsdp'), may hold values from -6 to 6
- norm_gain: float32 [16, 4096], P('section'), may hold values from 0.1 to 1.9
- key_grad: bfloat16 [4, 16, 1024, 512], P('island', 'section', 'fsdp'), may hold values from -18 to 18
- local_weight: bfloat16 [4, 16, 4096, 512], P('island', 'section', 'fsdp'), may hold values from -0.09375 to 0.09375
- drift: float32 [4, 16, 4096, 512], P('island', 'section', 'fsdp'), may hold values from -6 to 6
- momentum: float32 [16, 256, 4096], P('section', 'island', 'fsdp'), may hold values from -12 to 12
- seeds: int32 [16], P('section'), may hold values from 0 to 999999
Outputs:
- input_grad: bfloat16 [4, 16, 1024, 4096], P('island', 'section', 'fsdp')
- new_momentum: float32 [16, 256, 4096], P('section', 'island', 'fsdp')
- outer_update: float32 [16, 4096, 512], P('section', 'fsdp')
The draws below stay inside these ranges and needn't reach their ends.
All inputs are finite; a program needn't handle non-finite values.
Results may differ from the reference program's by a relative error of at most 0.014.
Values may be sent and summed in bfloat16 or wider, within the bound.
No kernel may reach another device: no remote copies, remote signals or barrier semaphores. Data moves between devices by JAX's collectives and lax.ppermute only.
A program may use at most 128 MiB of HBM per device.

```python
import math
import jax
import jax.numpy as jnp
from jax import lax

D = 4096
KV = 512
RANK = 256
TOK_DEV = 128
TOKENS = 1024
SECTIONS = 16
ISLANDS = 4
N_FSDP = 8


def plant(values, stream_key, low, top_value):
    longest = values.shape.index(max(values.shape))
    spots = []
    for shift in (0, 1):
        where = [jax.random.randint(jax.random.fold_in(stream_key, axis), (), 0, length) for axis, length in enumerate(values.shape)]
        where[longest] = (where[longest] + shift) % values.shape[longest]
        spots.append(tuple(where))
    return values.at[spots[0]].set(low).at[spots[1]].set(top_value)


def steps_of(own_key, shape, shards, low, top_value):
    gain, own = 1.0, jax.random.fold_in(own_key, 6)
    for axis_at, shards_of in shards:
        heights = jnp.exp(jax.random.uniform(jax.random.fold_in(own, axis_at), (shards_of,), jnp.float32, low / len(shards), top_value / len(shards)))
        gain = gain * jnp.repeat(heights, shape[axis_at] // shards_of).reshape([-1 if axis == axis_at else 1 for axis in range(len(shape))])
    return gain


def centred(rng, dims, spread, reach, split=(), kind=jnp.bfloat16):
    factor_of = steps_of(rng, dims, split, -0.22, 0.18) if split else 1.0
    values = jax.random.normal(rng, dims, jnp.float32) * spread * factor_of
    return jnp.minimum(jnp.maximum(values, -reach), reach).astype(kind)


def setup_inputs(seed: int = 0) -> dict:
    streams_of = jax.random.split(jax.random.key(seed), 8)
    hidden = centred(streams_of[0], (ISLANDS, SECTIONS, TOKENS, D), 1.0, 6.0, ((0, 4), (1, 16), (2, 8)))
    norm_gain = jnp.clip(1.0 + 0.18 * jax.random.normal(streams_of[1], (SECTIONS, D), jnp.float32), 0.1, 1.9)
    key_grad = centred(streams_of[2], (ISLANDS, SECTIONS, TOKENS, KV), 3.0, 18.0, ((0, 4), (1, 16), (2, 8)))
    local_weight = centred(streams_of[3], (ISLANDS, SECTIONS, D, KV), D ** -0.5, 0.09375, ((0, 4), (1, 16), (2, 8)))
    drift = centred(streams_of[4], (ISLANDS, SECTIONS, D, KV), 1.0, 6.0, ((0, 4), (1, 16), (2, 8)), jnp.float32)
    momentum = centred(streams_of[5], (SECTIONS, RANK, D), 2.0, 12.0, ((0, 16), (1, 4), (2, 8)), jnp.float32)
    seeds = plant(jax.random.randint(streams_of[6], (SECTIONS,), 0, 1000000), jax.random.fold_in(streams_of[6], 1), 0, 999999).astype(jnp.int32)
    return dict(hidden=hidden, norm_gain=norm_gain, key_grad=key_grad, local_weight=local_weight, drift=drift, momentum=momentum, seeds=seeds)


inner_rate = 0.01
outer_rate = 0.7
momentum_rate = 0.9

def projection_basis(seed_value, row_count, column_count):
    row_index = lax.broadcasted_iota(jnp.int32, (row_count, column_count), 0)
    column_index = lax.broadcasted_iota(jnp.int32, (row_count, column_count), 1)
    hashed = row_index * column_count + column_index + seed_value * 7919
    hashed = hashed * 1664525 + 1013904223 & 2147483647
    hashed = hashed ^ hashed >> 15
    hashed = hashed * 1103515245 + 12345 & 2147483647
    hashed = hashed ^ hashed >> 13
    levels = (hashed & 65535).astype(jnp.float32)
    return (levels - 32767.5) * (math.sqrt(12.0 / column_count) / 65536.0)

def reference(hidden, norm_gain, key_grad, local_weight, drift, momentum, seeds):
    bases = jax.vmap(lambda seed_value: projection_basis(seed_value, KV, RANK))(seeds)

    def per_section(items):
        section_hidden, section_keys, section_weight, section_drift, gain_row, basis_row = items
        values = section_hidden.astype(jnp.float32)
        recip = lax.rsqrt(lax.optimization_barrier(jnp.mean(values * values, -1, keepdims=True)) + 1e-05)
        unit = values * recip
        normed = (unit * gain_row).astype(jnp.bfloat16)
        key_back = jnp.dot(section_keys, section_weight.T, preferred_element_type=jnp.float32)
        scaled = gain_row * key_back
        branch = recip * (scaled - unit * lax.optimization_barrier(jnp.mean(scaled * unit, -1, keepdims=True)))
        block_norm = normed.reshape(N_FSDP, TOK_DEV, D).astype(jnp.float32)
        block_keys = section_keys.reshape(N_FSDP, TOK_DEV, KV).astype(jnp.float32)
        partial_grads = jnp.einsum('jtd,jtk->jdk', block_norm, block_keys).astype(jnp.bfloat16)
        weight_grad = lax.optimization_barrier(jnp.sum(partial_grads.astype(jnp.float32), 0))
        delta = section_drift + inner_rate * weight_grad
        factor = jnp.einsum('kr,dk->rd', basis_row, delta, precision=lax.Precision.HIGHEST)
        return (branch, factor)

    def per_island(items):
        island_hidden, island_keys, island_weight, island_drift = items
        branches, factors = lax.map(per_section, (island_hidden, island_keys, island_weight, island_drift, norm_gain, bases))
        suffix = jnp.cumsum(branches[::-1], axis=0)[::-1]
        return (suffix.astype(jnp.bfloat16), factors)
    input_grad, factors = lax.map(per_island, (hidden, key_grad, local_weight, drift))
    mean_factor = lax.optimization_barrier(jnp.sum(factors, 0)) / ISLANDS
    new_momentum = momentum_rate * momentum + mean_factor
    step_factor = mean_factor + momentum_rate * new_momentum
    outer_update = outer_rate * jnp.einsum('srd,skr->sdk', step_factor, bases, precision=lax.Precision.HIGHEST)
    return (input_grad, new_momentum, outer_update)
```

```python
import math

import jax
import jax.numpy as jnp
from jax import lax
from jax.experimental import pallas as pl
from jax.experimental.pallas import tpu as pltpu
from jax.sharding import PartitionSpec as P

RANK = 256


inner_rate = 0.01
outer_rate = 0.7
momentum_rate = 0.9


def projection_basis(seed_value, row_count, column_count):
    row_index = lax.broadcasted_iota(jnp.int32, (row_count, column_count), 0)
    column_index = lax.broadcasted_iota(jnp.int32, (row_count, column_count), 1)
    hashed = row_index * column_count + column_index + seed_value * 7919
    hashed = hashed * 1664525 + 1013904223 & 2147483647
    hashed = hashed ^ hashed >> 15
    hashed = hashed * 1103515245 + 12345 & 2147483647
    hashed = hashed ^ hashed >> 13
    levels = (hashed & 65535).astype(jnp.float32)
    return (levels - 32767.5) * (math.sqrt(12.0 / column_count) / 65536.0)


def suffix_kernel(parts_ref, sums_ref):
    count, _, width = parts_ref.shape
    step = 512

    def chunk(place, carry):
        span = pl.ds(pl.multiple_of(place * step, step), step)
        total = parts_ref[count - 1, :, span].astype(jnp.float32)
        sums_ref[count - 1, :, span] = total.astype(sums_ref.dtype)
        for source in range(count - 2, -1, -1):
            total = total + parts_ref[source, :, span].astype(jnp.float32)
            sums_ref[source, :, span] = total.astype(sums_ref.dtype)
        return carry

    lax.fori_loop(0, width // step, chunk, 0)


def suffix_sums(parts):
    return pl.pallas_call(
        suffix_kernel,
        out_shape=jax.ShapeDtypeStruct(parts.shape, parts.dtype),
        in_specs=[pl.BlockSpec(memory_space=pltpu.VMEM)],
        out_specs=pl.BlockSpec(memory_space=pltpu.VMEM),
        compiler_params=pltpu.CompilerParams(vmem_limit_bytes=16 * 1024 * 1024),
        name="suffix_sums",
    )(parts)


def shards(hidden, norm_gain, key_grad, local_weight, drift, momentum, seeds):
    tokens, width = hidden.shape[2:]
    sections = lax.axis_size("section")
    islands = lax.axis_size("island")
    weight = lax.all_gather(local_weight[0, 0], "fsdp", axis=0, tiled=True)
    values = hidden[0, 0].astype(jnp.float32)
    gain_row = norm_gain[0]
    section_keys = key_grad[0, 0]
    key_width = section_keys.shape[1]
    recip = lax.rsqrt(jnp.mean(values * values, -1, keepdims=True) + 1e-05)
    unit = values * recip
    normed = (unit * gain_row).astype(jnp.bfloat16)

    basis_row = projection_basis(seeds[0], key_width, RANK)
    projected_keys = jnp.dot(
        section_keys.astype(jnp.float32), basis_row, precision=lax.Precision.HIGHEST
    ).astype(jnp.bfloat16)
    partial_factor = lax.dot_general(
        projected_keys, normed, (((0,), (0,)), ((), ())), preferred_element_type=jnp.float32
    ).astype(jnp.bfloat16)
    drift_factor = jnp.einsum("kr,dk->rd", basis_row, drift[0, 0], precision=lax.Precision.HIGHEST)
    all_momentum = lax.all_gather(momentum[0], "island", axis=0, tiled=True)

    key_back = lax.dot_general(
        section_keys, weight, (((1,), (1,)), ((), ())), preferred_element_type=jnp.float32
    )
    scaled = gain_row * key_back
    branch = recip * (scaled - unit * jnp.mean(scaled * unit, -1, keepdims=True))
    pieces = branch.astype(jnp.bfloat16).reshape(sections, tokens // sections, width)
    pieces = lax.all_to_all(pieces, "section", 0, 0)
    pieces = lax.all_to_all(suffix_sums(pieces), "section", 0, 0)
    input_grad = pieces.reshape(tokens, width)

    gradient_factor = lax.psum_scatter(partial_factor, "fsdp", scatter_dimension=1, tiled=True)
    factor = drift_factor + inner_rate * gradient_factor.astype(jnp.float32)
    total_factor = lax.psum(factor.astype(jnp.bfloat16), "island").astype(jnp.float32)
    mean_factor = total_factor / islands
    next_momentum = momentum_rate * all_momentum + mean_factor
    step_factor = mean_factor + momentum_rate * next_momentum
    rank_share = momentum.shape[1]
    own_momentum = lax.dynamic_slice_in_dim(
        next_momentum, lax.axis_index("island") * rank_share, rank_share, 0
    )
    outer_update = outer_rate * jnp.einsum(
        "rd,kr->dk", step_factor, basis_row, precision=lax.Precision.HIGHEST
    )
    return (input_grad[None, None], own_momentum[None], outer_update[None])


def solution(mesh):
    return jax.shard_map(
        shards,
        mesh=mesh,
        in_specs=(
            P("island", "section", "fsdp", None),
            P("section", None),
            P("island", "section", "fsdp", None),
            P("island", "section", "fsdp", None),
            P("island", "section", "fsdp", None),
            P("section", "island", "fsdp"),
            P("section"),
        ),
        out_specs=(
            P("island", "section", "fsdp", None),
            P("section", "island", "fsdp"),
            P("section", "fsdp", None),
        ),
        check_vma=False,
    )
```

```python
import math

import jax
import jax.numpy as jnp
from jax import lax
from jax.experimental import pallas as pl
from jax.experimental.pallas import tpu as pltpu
from jax.sharding import PartitionSpec as P

RANK = 256
CORES = 2


inner_rate = 0.01
outer_rate = 0.7
momentum_rate = 0.9


def projection_basis(seed_value, row_count, column_count):
    row_index = lax.broadcasted_iota(jnp.int32, (row_count, column_count), 0)
    column_index = lax.broadcasted_iota(jnp.int32, (row_count, column_count), 1)
    hashed = row_index * column_count + column_index + seed_value * 7919
    hashed = hashed * 1664525 + 1013904223 & 2147483647
    hashed = hashed ^ hashed >> 15
    hashed = hashed * 1103515245 + 12345 & 2147483647
    hashed = hashed ^ hashed >> 13
    levels = (hashed & 65535).astype(jnp.float32)
    return (levels - 32767.5) * (math.sqrt(12.0 / column_count) / 65536.0)


def whole_vmem():
    return pl.BlockSpec(memory_space=pltpu.VMEM)


def whole_hbm():
    return pl.BlockSpec(memory_space=pltpu.HBM)


def in_hbm(array):
    return pltpu.with_memory_space_constraint(array, pltpu.HBM)


def kernel_params():
    return pltpu.CompilerParams(vmem_limit_bytes=24 * 1024 * 1024)


def suffix_kernel(parts_ref, sums_ref, out, out_sems):
    chunks, count, _, step = out.shape

    def departure(place):
        span = pl.ds(place * step, step)
        return pltpu.make_async_copy(out.at[place], sums_ref.at[:, :, span], out_sems.at[place])

    for place in range(chunks):
        span = pl.ds(place * step, step)
        total = parts_ref[count - 1, :, span].astype(jnp.float32)
        out[place, count - 1] = total.astype(out.dtype)
        for source in range(count - 2, -1, -1):
            total = total + parts_ref[source, :, span].astype(jnp.float32)
            out[place, source] = total.astype(out.dtype)
        departure(place).start()
    for place in range(chunks):
        departure(place).wait()


def suffix_sums(parts):
    count, rows, width = parts.shape
    step = 512
    chunks = width // step
    return pl.pallas_call(
        suffix_kernel,
        out_shape=pltpu.HBM(parts.shape, parts.dtype),
        in_specs=[whole_vmem()],
        out_specs=whole_hbm(),
        scratch_shapes=[
            pltpu.VMEM((chunks, count, rows, step), parts.dtype),
            pltpu.SemaphoreType.DMA((chunks,)),
        ],
        compiler_params=kernel_params(),
        name="suffix_sums",
    )(pltpu.with_memory_space_constraint(parts, pltpu.VMEM))


def key_back_kernel(
    core_ref, keys_ref, own_ref, other_ref, back_ref, held, out, held_sem, out_sems
):
    chips = keys_ref.shape[0]
    width = own_ref.shape[0]
    core = core_ref[0]
    arrival = pltpu.make_async_copy(other_ref.at[pl.ds(0, width)], held, held_sem)
    arrival.start()

    def departure(chip):
        return pltpu.make_async_copy(out.at[chip], back_ref.at[chip], out_sems.at[chip])

    for weight_ref, place in ((own_ref, core), (held, 1 - core)):
        span = pl.ds(pl.multiple_of(place * width, width), width)
        if weight_ref is held:
            arrival.wait()
        for chip in range(chips):
            out[chip, :, span] = lax.dot_general(
                keys_ref[chip],
                weight_ref[...],
                (((1,), (1,)), ((), ())),
                preferred_element_type=jnp.float32,
            ).astype(out.dtype)
            if weight_ref is held:
                departure(chip).start()
    for chip in range(chips):
        departure(chip).wait()


def key_back_columns(core, keys, own_weight, arrived):
    chips, tokens, _ = keys.shape
    shape = (chips, tokens, CORES * own_weight.shape[0])
    return pl.pallas_call(
        key_back_kernel,
        out_shape=pltpu.HBM(shape, jnp.bfloat16),
        in_specs=[pl.BlockSpec(memory_space=pltpu.SMEM), whole_vmem(), whole_vmem(), whole_hbm()],
        out_specs=whole_hbm(),
        scratch_shapes=[
            pltpu.VMEM(own_weight.shape, own_weight.dtype),
            pltpu.VMEM(shape, jnp.bfloat16),
            pltpu.SemaphoreType.DMA,
            pltpu.SemaphoreType.DMA((chips,)),
        ],
        compiler_params=kernel_params(),
        name="key_back_columns",
    )(core.reshape(1), keys, own_weight, in_hbm(arrived))


def prepare_kernel(
    core_ref,
    hidden_ref,
    gain_ref,
    weight_ref,
    own_ref,
    swap_ref,
    held,
    own_out,
    swap_out,
    weight,
    held_sems,
    own_sems,
    swap_sems,
):
    tokens, width = hidden_ref.shape
    chips, _, slice_width = own_ref.shape
    chunks = held_sems.shape[0] - 1
    core = core_ref[0]
    rows = 16
    each = tokens // chunks

    def arrival(chunk):
        lines = pl.ds(chunk * each, each)
        return pltpu.make_async_copy(hidden_ref.at[lines], held.at[lines], held_sems.at[chunk])

    weight_in = pltpu.make_async_copy(weight_ref, weight, held_sems.at[chunks])
    weight_out = pltpu.make_async_copy(
        weight, swap_ref.at[pl.ds(0, slice_width)], swap_sems.at[chips]
    )
    for chunk in range(chunks):
        arrival(chunk).start()
    weight_in.start()

    def group(place, carry):
        lines = pl.ds(pl.multiple_of(place * rows, rows), rows)
        squares = jnp.zeros((rows, 128), jnp.float32)
        for at in range(0, width, 128):
            value = held[lines, at : at + 128].astype(jnp.float32)
            squares = squares + value * value
        recip = lax.rsqrt(jnp.sum(squares, -1, keepdims=True) / width + 1e-05)

        def normed(chip, side):
            at = pl.multiple_of((CORES * chip + side) * slice_width, slice_width)
            span = pl.ds(at, slice_width)
            value = held[lines, span].astype(jnp.float32) * recip
            return (value * gain_ref[:, span]).astype(own_out.dtype)

        for chip in range(chips):
            own_out[chip, lines, :] = normed(chip, core)
            swap_out[chip, lines, :] = normed(chip, 1 - core)
        return carry

    for chunk in range(chunks):
        arrival(chunk).wait()
        lax.fori_loop(chunk * each // rows, (chunk + 1) * each // rows, group, 0)
        if chunk == 0:
            weight_in.wait()
            weight_out.start()

    def departures(chip):
        at = slice_width + chip * tokens
        return (
            pltpu.make_async_copy(
                swap_out.at[chip], swap_ref.at[pl.ds(at, tokens)], swap_sems.at[chip]
            ),
            pltpu.make_async_copy(own_out.at[chip], own_ref.at[chip], own_sems.at[chip]),
        )

    for chip in range(chips):
        for copy in departures(chip):
            copy.start()
    weight_out.wait()
    for chip in range(chips):
        for copy in departures(chip):
            copy.wait()


def prepare(core, hidden, gain_row, weight):
    tokens, width = hidden.shape
    slice_width, key_width = weight.shape
    chips = width // slice_width // CORES
    chunks = 4
    columns = (chips, tokens, slice_width)
    return pl.pallas_call(
        prepare_kernel,
        out_shape=(
            pltpu.HBM(columns, jnp.bfloat16),
            pltpu.HBM((slice_width + chips * tokens, key_width), jnp.bfloat16),
        ),
        in_specs=[
            pl.BlockSpec(memory_space=pltpu.SMEM),
            whole_hbm(),
            whole_vmem(),
            whole_hbm(),
        ],
        out_specs=(whole_hbm(),) * 2,
        scratch_shapes=[
            pltpu.VMEM(hidden.shape, hidden.dtype),
            pltpu.VMEM(columns, jnp.bfloat16),
            pltpu.VMEM(columns, jnp.bfloat16),
            pltpu.VMEM(weight.shape, weight.dtype),
            pltpu.SemaphoreType.DMA((chunks + 1,)),
            pltpu.SemaphoreType.DMA((chips,)),
            pltpu.SemaphoreType.DMA((chips + 1,)),
        ],
        compiler_params=kernel_params(),
        name="prepare",
    )(core.reshape(1), in_hbm(hidden), gain_row, in_hbm(weight))


def pair_kernel(chip_ref, own_ref, other_ref, *refs):
    part_refs, (held, in_sems, out_sems) = refs[:-3], refs[-3:]
    chips, tokens, _ = own_ref.shape
    first = other_ref.shape[0] - chips * tokens
    arrivals, departures = [], []
    for turn, part_ref in enumerate(part_refs):
        target = lax.rem(chip_ref[0] + turn, chips)
        lines = pl.ds(pl.multiple_of(first + target * tokens, tokens), tokens)
        for side, source in enumerate((own_ref.at[target], other_ref.at[lines])):
            place = held.at[turn, side]
            arrivals.append(pltpu.make_async_copy(source, place, in_sems.at[turn, side]))
            departures.append(
                pltpu.make_async_copy(place, part_ref.at[side], out_sems.at[turn, side])
            )
    for copy in arrivals:
        copy.start()
    for arrival, departure in zip(arrivals, departures, strict=True):
        arrival.wait()
        departure.start()
    for copy in departures:
        copy.wait()


def pair_columns(chip, own_normed, arrived):
    chips, tokens, slice_width = own_normed.shape
    shape = (CORES, tokens, slice_width)
    return pl.pallas_call(
        pair_kernel,
        out_shape=(pltpu.HBM(shape, own_normed.dtype),) * chips,
        in_specs=[pl.BlockSpec(memory_space=pltpu.SMEM)] + [whole_hbm()] * 2,
        out_specs=(whole_hbm(),) * chips,
        scratch_shapes=[
            pltpu.VMEM((chips, *shape), own_normed.dtype),
            pltpu.SemaphoreType.DMA((chips, CORES)),
            pltpu.SemaphoreType.DMA((chips, CORES)),
        ],
        compiler_params=kernel_params(),
        name="pair_columns",
    )(chip.reshape(1), in_hbm(own_normed), in_hbm(arrived))


def factor_kernel(chip_ref, own_keys, other_keys, drift_ref, part0, part1, part2, part3, sum_ref):
    chips = own_keys.shape[0]
    total = jnp.zeros(sum_ref.shape, jnp.float32)
    for turn, part_ref in enumerate((part0, part1, part2, part3)):
        source = lax.rem(chip_ref[0] + (chips - turn), chips)
        for side, keys_ref in enumerate((own_keys, other_keys)):
            total = total + lax.dot_general(
                keys_ref[source],
                part_ref[side],
                (((0,), (0,)), ((), ())),
                preferred_element_type=jnp.float32,
            )
    sum_ref[...] = drift_ref[...] + inner_rate * total


def factor_columns(chip, own_keys, other_keys, drift_factor, parts):
    return pl.pallas_call(
        factor_kernel,
        out_shape=jax.ShapeDtypeStruct(drift_factor.shape, jnp.float32),
        in_specs=[pl.BlockSpec(memory_space=pltpu.SMEM)] + [whole_vmem()] * 7,
        out_specs=whole_vmem(),
        compiler_params=kernel_params(),
        name="factor_columns",
    )(chip.reshape(1), own_keys, other_keys, drift_factor, *parts)


def branch_kernel(hidden_ref, back_ref, gain_ref, pieces_ref, out, out_sem):
    tokens, width = hidden_ref.shape
    chips, _, span = back_ref.shape
    rows = 16
    count = pieces_ref.shape[1]
    each = rows // count

    def departure(place):
        run = pl.ds(place * each, each)
        return pltpu.make_async_copy(out.at[run], pieces_ref.at[run], out_sem)

    def group(place, carry):
        lines = pl.ds(pl.multiple_of(place * rows, rows), rows)
        squares = jnp.zeros((rows, 128), jnp.float32)
        cross = jnp.zeros((rows, 128), jnp.float32)
        for chip in range(chips):
            for column in range(0, span, 128):
                at = chip * span + column
                value = hidden_ref[lines, at : at + 128].astype(jnp.float32)
                back = back_ref[chip, lines, column : column + 128].astype(jnp.float32)
                squares = squares + value * value
                cross = cross + value * (back * gain_ref[:, at : at + 128])
        recip = lax.rsqrt(jnp.sum(squares, -1, keepdims=True) / width + 1e-05)
        mean = jnp.sum(cross, -1, keepdims=True) * recip / width
        share = recip * recip * mean
        for chip in range(chips):
            for column in range(0, span, 128):
                at = chip * span + column
                value = hidden_ref[lines, at : at + 128].astype(jnp.float32)
                back = back_ref[chip, lines, column : column + 128].astype(jnp.float32)
                branch = recip * (back * gain_ref[:, at : at + 128]) - share * value
                branch = branch.astype(out.dtype)
                for part in range(each):
                    lines_of = branch[part * count : (part + 1) * count]
                    out[place * each + part, :, at : at + 128] = lines_of
        departure(place).start()
        return carry

    lax.fori_loop(0, tokens // rows, group, 0)
    pltpu.make_async_copy(out, pieces_ref, out_sem).wait()


def branch_pieces(hidden, back, gain_row, sections):
    tokens, width = hidden.shape
    shape = (sections, tokens // sections, width)
    return pl.pallas_call(
        branch_kernel,
        out_shape=pltpu.HBM(shape, jnp.bfloat16),
        in_specs=[whole_vmem()] * 3,
        out_specs=whole_hbm(),
        scratch_shapes=[pltpu.VMEM(shape, jnp.bfloat16), pltpu.SemaphoreType.DMA],
        compiler_params=kernel_params(),
        name="branch_pieces",
    )(pltpu.with_memory_space_constraint(hidden, pltpu.VMEM), back, gain_row)


def shards(hidden, norm_gain, key_grad, local_weight, drift, momentum, seeds):
    tokens, width = hidden.shape[2:]
    sections = lax.axis_size("section")
    islands = lax.axis_size("island")
    lanes = lax.axis_size("fsdp")
    chips = lanes // CORES
    lane = lax.axis_index("fsdp")
    chip, core = lane // CORES, lane - lane // CORES * CORES
    swap = [(i, i ^ 1) for i in range(lanes)]
    x_lines = [[c + CORES * i for i in range(chips)] for c in range(CORES)]
    gain_row = norm_gain
    own_hidden = hidden[0, 0]
    own_weight = local_weight[0, 0]
    slice_width = own_weight.shape[0]
    span = CORES * slice_width

    own_normed, swapped = prepare(core, own_hidden, gain_row, own_weight)
    swapped, sent_keys = lax.optimization_barrier((swapped, key_grad[0, 0]))
    arrived = lax.ppermute(swapped, "fsdp", swap)
    line_keys = lax.all_gather(sent_keys, "fsdp", axis_index_groups=x_lines)
    back = key_back_columns(core, line_keys, own_weight, arrived)
    back, own_normed, arrived = lax.optimization_barrier((back, own_normed, arrived))
    back = lax.all_to_all(back, "fsdp", 0, 0, axis_index_groups=x_lines)
    parts = list(pair_columns(chip, own_normed, arrived))
    for turn in (2, 1, 3):
        path = [(i, (i + CORES * turn) % lanes) for i in range(lanes)]
        parts[turn] = lax.ppermute(parts[turn], "fsdp", path)
    pieces = branch_pieces(own_hidden, back, gain_row, sections)
    pieces, *parts = lax.optimization_barrier((pieces, *parts))

    pieces = lax.all_to_all(pieces, "section", 0, 0)

    basis_row = projection_basis(seeds[0], line_keys.shape[2], RANK)
    own_keys = lax.dot_general(
        line_keys,
        basis_row.astype(jnp.bfloat16),
        (((2,), (0,)), ((), ())),
        preferred_element_type=jnp.float32,
    ).astype(jnp.bfloat16)
    other_keys = lax.ppermute(own_keys, "fsdp", swap)
    drift_factor = jnp.einsum("kr,dk->rd", basis_row, drift[0, 0], precision=lax.Precision.HIGH)
    factor = factor_columns(chip, own_keys, other_keys, drift_factor, parts)
    rank_share = momentum.shape[1]
    island = lax.axis_index("island")

    def rows_of(flip):
        at = jnp.bitwise_xor(island, flip) * rank_share
        return lax.dynamic_slice_in_dim(factor, at, rank_share, 0)

    def exchange(rows, flip):
        path = [(i, i ^ flip) for i in range(islands)]
        return lax.ppermute(rows.astype(jnp.bfloat16), "island", path).astype(jnp.float32)

    rows = exchange(jnp.concatenate([rows_of(1), rows_of(2)]), 1)
    own_sum = rows_of(0) + rows[:rank_share]
    other_sum = rows_of(3) + rows[rank_share:]
    pieces, own_sum, other_sum = lax.optimization_barrier((pieces, own_sum, other_sum))
    pieces = lax.all_to_all(suffix_sums(pieces), "section", 0, 0)
    input_grad = pieces.reshape(tokens, width)

    own_mean = (own_sum + exchange(other_sum, 3)) / islands
    own_momentum = momentum_rate * momentum[0] + own_mean
    own_step = (own_mean + momentum_rate * own_momentum).astype(jnp.bfloat16)
    step_factor = lax.all_gather(own_step, "island", axis=0, tiled=True).astype(jnp.float32)
    outer_update = outer_rate * jnp.einsum(
        "rd,kr->dk", step_factor, basis_row, precision=lax.Precision.HIGH
    )
    return (input_grad[None, None], own_momentum[None], outer_update[None])


def solution(mesh):
    return jax.shard_map(
        shards,
        mesh=mesh,
        in_specs=(
            P("island", "section", "fsdp", None),
            P("section", None),
            P("island", "section", "fsdp", None),
            P("island", "section", "fsdp", None),
            P("island", "section", "fsdp", None),
            P("section", "island", "fsdp"),
            P("section"),
        ),
        out_specs=(
            P("island", "section", "fsdp", None),
            P("section", "island", "fsdp"),
            P("section", "fsdp", None),
        ),
        check_vma=False,
    )
```

```python
import math

import jax
import jax.numpy as jnp
from jax import lax
from jax.experimental import pallas as pl
from jax.experimental.pallas import tpu as pltpu
from jax.sharding import PartitionSpec as P

RANK = 256
CORES = 2


inner_rate = 0.01
outer_rate = 0.7
momentum_rate = 0.9


def projection_basis(seed_value, row_count, column_count):
    row_index = lax.broadcasted_iota(jnp.int32, (row_count, column_count), 0)
    column_index = lax.broadcasted_iota(jnp.int32, (row_count, column_count), 1)
    hashed = row_index * column_count + column_index + seed_value * 7919
    hashed = hashed * 1664525 + 1013904223 & 2147483647
    hashed = hashed ^ hashed >> 15
    hashed = hashed * 1103515245 + 12345 & 2147483647
    hashed = hashed ^ hashed >> 13
    levels = (hashed & 65535).astype(jnp.float32)
    return (levels - 32767.5) * (math.sqrt(12.0 / column_count) / 65536.0)


def whole_vmem():
    return pl.BlockSpec(memory_space=pltpu.VMEM)


def whole_hbm():
    return pl.BlockSpec(memory_space=pltpu.HBM)


def anywhere():
    return pl.BlockSpec(memory_space=pl.ANY)


def in_vmem(array):
    return pltpu.with_memory_space_constraint(array, pltpu.VMEM)


def in_hbm(array):
    return pltpu.with_memory_space_constraint(array, pltpu.HBM)


def kernel_params():
    return pltpu.CompilerParams(vmem_limit_bytes=8 * 1024 * 1024)


def suffix_kernel(parts_ref, sums_ref, out, out_sems):
    chunks, count, _, step = out.shape

    def departure(place):
        span = pl.ds(place * step, step)
        return pltpu.make_async_copy(out.at[place], sums_ref.at[:, :, span], out_sems.at[place])

    for place in range(chunks):
        span = pl.ds(place * step, step)
        total = parts_ref[count - 1, :, span].astype(jnp.float32)
        out[place, count - 1] = total.astype(out.dtype)
        for source in range(count - 2, -1, -1):
            total = total + parts_ref[source, :, span].astype(jnp.float32)
            out[place, source] = total.astype(out.dtype)
        departure(place).start()
    for place in range(chunks):
        departure(place).wait()


def suffix_sums(parts):
    count, rows, width = parts.shape
    step = 512
    chunks = width // step
    return pl.pallas_call(
        suffix_kernel,
        out_shape=pltpu.HBM(parts.shape, parts.dtype),
        in_specs=[whole_vmem()],
        out_specs=whole_hbm(),
        scratch_shapes=[
            pltpu.VMEM((chunks, count, rows, step), parts.dtype),
            pltpu.SemaphoreType.DMA((chunks,)),
        ],
        compiler_params=kernel_params(),
        name="suffix_sums",
    )(pltpu.with_memory_space_constraint(parts, pltpu.VMEM))


def key_back_kernel(core_ref, keys_ref, own_ref, other_ref, back_ref, out, out_sems):
    chips, tokens, depth = keys_ref.shape
    width = own_ref.shape[0]
    core = core_ref[0]
    keys = keys_ref[...].reshape(chips * tokens, depth)

    def departure(side, chip):
        span = pl.ds(pl.multiple_of((core if side == 0 else 1 - core) * width, width), width)
        return pltpu.make_async_copy(
            out.at[side, chip], back_ref.at[chip, :, span], out_sems.at[side, chip]
        )

    for side, weight_ref in enumerate((own_ref, other_ref)):
        product = lax.dot_general(
            keys,
            weight_ref[0:width, :],
            (((1,), (1,)), ((), ())),
            preferred_element_type=jnp.float32,
        ).astype(out.dtype)
        for chip in range(chips):
            out[side, chip] = product[chip * tokens : (chip + 1) * tokens]
            departure(side, chip).start()
    for side in range(CORES):
        for chip in range(chips):
            departure(side, chip).wait()


def key_back_columns(core, keys, own_weight, arrived):
    chips, tokens, _ = keys.shape
    width = own_weight.shape[0]
    return pl.pallas_call(
        key_back_kernel,
        out_shape=pltpu.HBM((chips, tokens, CORES * width), jnp.bfloat16),
        in_specs=[pl.BlockSpec(memory_space=pltpu.SMEM)] + [whole_vmem()] * 3,
        out_specs=whole_hbm(),
        scratch_shapes=[
            pltpu.VMEM((CORES, chips, tokens, width), jnp.bfloat16),
            pltpu.SemaphoreType.DMA((CORES, chips)),
        ],
        compiler_params=kernel_params(),
        name="key_back_columns",
    )(core.reshape(1), keys, own_weight, arrived)


def prepare_kernel(
    core_ref,
    hidden_ref,
    gain_ref,
    weight_ref,
    own_ref,
    swap_ref,
    held,
    gain,
    outs,
    weight,
    held_sems,
    out_sems,
):
    tokens, width = hidden_ref.shape
    chips, _, slice_width = own_ref.shape
    chunks = out_sems.shape[1]
    core = core_ref[0]
    rows = tokens // chunks

    def arrival(chunk):
        lines = pl.ds(chunk * rows, rows)
        return pltpu.make_async_copy(hidden_ref.at[lines], held.at[lines], held_sems.at[chunk])

    def departures(chunk):
        lines = pl.ds(chunk * rows, rows)
        for chip in range(chips):
            below = pl.ds(slice_width + chip * tokens + chunk * rows, rows)
            for side, place in enumerate((own_ref.at[chip, lines], swap_ref.at[below])):
                yield pltpu.make_async_copy(
                    outs.at[side, chip, lines], place, out_sems.at[side, chunk, chip]
                )

    gain_in = pltpu.make_async_copy(gain_ref, gain, held_sems.at[chunks])
    weight_in = pltpu.make_async_copy(weight_ref, weight, held_sems.at[chunks + 1])
    weight_out = pltpu.make_async_copy(
        weight, swap_ref.at[pl.ds(0, slice_width)], held_sems.at[chunks + 2]
    )
    arrival(0).start()
    gain_in.start()
    for chunk in range(1, chunks):
        arrival(chunk).start()
    weight_in.start()
    gain_in.wait()
    for chunk in range(chunks):
        arrival(chunk).wait()
        lines = pl.ds(chunk * rows, rows)
        squares = [jnp.zeros((rows, 128), jnp.float32)] * 2
        for column in range(0, width // 128):
            value = held[lines, column * 128 : column * 128 + 128].astype(jnp.float32)
            squares[column % 2] = squares[column % 2] + value * value
        total = jnp.sum(squares[0] + squares[1], -1, keepdims=True)
        recip = lax.rsqrt(total / width + 1e-05)
        for chip in range(chips):
            for side, place in enumerate((core, 1 - core)):
                first = pl.multiple_of((CORES * chip + place) * slice_width, slice_width)
                for column in range(0, slice_width, 128):
                    span = pl.ds(pl.multiple_of(first + column, 128), 128)
                    value = held[lines, span].astype(jnp.float32) * recip
                    normed = (value * gain[:, span]).astype(outs.dtype)
                    outs[side, chip, lines, column : column + 128] = normed
        for copy in departures(chunk):
            copy.start()
        if chunk == 0:
            weight_in.wait()
            weight_out.start()
    weight_out.wait()
    for chunk in range(chunks):
        for copy in departures(chunk):
            copy.wait()


def prepare(core, hidden, gain_row, weight):
    tokens, width = hidden.shape
    slice_width, key_width = weight.shape
    chips = width // slice_width // CORES
    chunks = 4
    columns = (chips, tokens, slice_width)
    return pl.pallas_call(
        prepare_kernel,
        out_shape=(
            pltpu.HBM(columns, jnp.bfloat16),
            pltpu.HBM((slice_width + chips * tokens, key_width), jnp.bfloat16),
        ),
        in_specs=[pl.BlockSpec(memory_space=pltpu.SMEM)] + [whole_hbm()] * 3,
        out_specs=(whole_hbm(),) * 2,
        scratch_shapes=[
            pltpu.VMEM(hidden.shape, hidden.dtype),
            pltpu.VMEM(gain_row.shape, gain_row.dtype),
            pltpu.VMEM((CORES, *columns), jnp.bfloat16),
            pltpu.VMEM(weight.shape, weight.dtype),
            pltpu.SemaphoreType.DMA((chunks + 3,)),
            pltpu.SemaphoreType.DMA((CORES, chunks, chips)),
        ],
        compiler_params=kernel_params(),
        name="prepare",
    )(core.reshape(1), in_hbm(hidden), in_hbm(gain_row), in_hbm(weight))


def pair_kernel(chip_ref, own_ref, other_ref, *refs):
    part_refs, (held, in_sems, out_sems) = refs[:-3], refs[-3:]
    chips, tokens, _ = own_ref.shape
    first = other_ref.shape[0] - chips * tokens
    arrivals, departures = [], []
    for turn, part_ref in enumerate(part_refs):
        target = lax.rem(chip_ref[0] + turn, chips)
        lines = pl.ds(pl.multiple_of(first + target * tokens, tokens), tokens)
        for side, source in enumerate((own_ref.at[target], other_ref.at[lines])):
            place = held.at[turn, side]
            arrivals.append(pltpu.make_async_copy(source, place, in_sems.at[turn, side]))
            departures.append(
                pltpu.make_async_copy(place, part_ref.at[side], out_sems.at[turn, side])
            )
    for copy in arrivals:
        copy.start()
    for arrival, departure in zip(arrivals, departures, strict=True):
        arrival.wait()
        departure.start()
    for copy in departures:
        copy.wait()


def pair_columns(chip, own_normed, arrived):
    chips, tokens, slice_width = own_normed.shape
    shape = (CORES, tokens, slice_width)
    return pl.pallas_call(
        pair_kernel,
        out_shape=(pltpu.HBM(shape, own_normed.dtype),) * chips,
        in_specs=[pl.BlockSpec(memory_space=pltpu.SMEM), whole_hbm(), anywhere()],
        out_specs=(whole_hbm(),) * chips,
        scratch_shapes=[
            pltpu.VMEM((chips, *shape), own_normed.dtype),
            pltpu.SemaphoreType.DMA((chips, CORES)),
            pltpu.SemaphoreType.DMA((chips, CORES)),
        ],
        compiler_params=kernel_params(),
        name="pair_columns",
    )(chip.reshape(1), in_hbm(own_normed), arrived)


def factor_kernel(chip_ref, own_keys, other_keys, drift_ref, part0, part1, part2, part3, sum_ref):
    chips = own_keys.shape[0]
    total = jnp.zeros(sum_ref.shape, jnp.float32)
    for turn, part_ref in enumerate((part0, part1, part2, part3)):
        source = lax.rem(chip_ref[0] + (chips - turn), chips)
        for side, keys_ref in enumerate((own_keys, other_keys)):
            total = total + lax.dot_general(
                keys_ref[source],
                part_ref[side],
                (((0,), (0,)), ((), ())),
                preferred_element_type=jnp.float32,
            )
    sum_ref[...] = drift_ref[...] + inner_rate * total


def factor_columns(chip, own_keys, other_keys, drift_factor, parts):
    return pl.pallas_call(
        factor_kernel,
        out_shape=jax.ShapeDtypeStruct(drift_factor.shape, jnp.float32),
        in_specs=[pl.BlockSpec(memory_space=pltpu.SMEM)] + [whole_vmem()] * 7,
        out_specs=whole_vmem(),
        compiler_params=kernel_params(),
        name="factor_columns",
    )(chip.reshape(1), own_keys, other_keys, drift_factor, *parts)


def branch_kernel(hidden_ref, back_ref, gain_ref, pieces_ref, out, out_sem):
    tokens, width = hidden_ref.shape
    chips, _, span = back_ref.shape
    rows = 16
    count = pieces_ref.shape[1]
    each = rows // count

    def departure(place):
        run = pl.ds(place * each, each)
        return pltpu.make_async_copy(out.at[run], pieces_ref.at[run], out_sem)

    def group(place, carry):
        lines = pl.ds(pl.multiple_of(place * rows, rows), rows)
        squares = jnp.zeros((rows, 128), jnp.float32)
        cross = jnp.zeros((rows, 128), jnp.float32)
        for chip in range(chips):
            for column in range(0, span, 128):
                at = chip * span + column
                value = hidden_ref[lines, at : at + 128].astype(jnp.float32)
                back = back_ref[chip, lines, column : column + 128].astype(jnp.float32)
                squares = squares + value * value
                cross = cross + value * (back * gain_ref[:, at : at + 128])
        recip = lax.rsqrt(jnp.sum(squares, -1, keepdims=True) / width + 1e-05)
        mean = jnp.sum(cross, -1, keepdims=True) * recip / width
        share = recip * recip * mean
        for chip in range(chips):
            for column in range(0, span, 128):
                at = chip * span + column
                value = hidden_ref[lines, at : at + 128].astype(jnp.float32)
                back = back_ref[chip, lines, column : column + 128].astype(jnp.float32)
                branch = recip * (back * gain_ref[:, at : at + 128]) - share * value
                branch = branch.astype(out.dtype)
                for part in range(each):
                    lines_of = branch[part * count : (part + 1) * count]
                    out[place * each + part, :, at : at + 128] = lines_of
        departure(place).start()
        return carry

    lax.fori_loop(0, tokens // rows, group, 0)
    pltpu.make_async_copy(out, pieces_ref, out_sem).wait()


def branch_pieces(hidden, back, gain_row, sections):
    tokens, width = hidden.shape
    shape = (sections, tokens // sections, width)
    return pl.pallas_call(
        branch_kernel,
        out_shape=pltpu.HBM(shape, jnp.bfloat16),
        in_specs=[whole_vmem()] * 3,
        out_specs=whole_hbm(),
        scratch_shapes=[pltpu.VMEM(shape, jnp.bfloat16), pltpu.SemaphoreType.DMA],
        compiler_params=kernel_params(),
        name="branch_pieces",
    )(pltpu.with_memory_space_constraint(hidden, pltpu.VMEM), back, gain_row)


def shards(hidden, norm_gain, key_grad, local_weight, drift, momentum, seeds):
    tokens, width = hidden.shape[2:]
    sections = lax.axis_size("section")
    islands = lax.axis_size("island")
    lanes = lax.axis_size("fsdp")
    chips = lanes // CORES
    lane = lax.axis_index("fsdp")
    chip, core = lane // CORES, lane - lane // CORES * CORES
    swap = [(i, i ^ 1) for i in range(lanes)]
    x_lines = [[c + CORES * i for i in range(chips)] for c in range(CORES)]
    gain_row = norm_gain
    own_hidden = hidden[0, 0]
    own_weight = local_weight[0, 0]
    slice_width = own_weight.shape[0]
    span = CORES * slice_width

    own_normed, swapped = prepare(core, own_hidden, gain_row, own_weight)
    swapped, sent_keys = lax.optimization_barrier((swapped, key_grad[0, 0]))
    arrived = lax.ppermute(swapped, "fsdp", swap)
    line_keys = lax.all_gather(sent_keys, "fsdp", axis_index_groups=x_lines)
    back = key_back_columns(core, line_keys, own_weight, arrived)
    back, own_normed, arrived = lax.optimization_barrier((back, own_normed, arrived))
    back = lax.all_to_all(back, "fsdp", 0, 0, axis_index_groups=x_lines)
    parts = list(pair_columns(chip, own_normed, arrived))
    basis_row = projection_basis(seeds[0], line_keys.shape[2], RANK)
    own_keys = lax.dot_general(
        line_keys,
        basis_row.astype(jnp.bfloat16),
        (((2,), (0,)), ((), ())),
        preferred_element_type=jnp.float32,
    ).astype(jnp.bfloat16)
    other_keys = lax.ppermute(own_keys, "fsdp", swap)
    back, own_keys, other_keys, *parts = lax.optimization_barrier(
        (back, own_keys, other_keys, *parts)
    )
    pieces = branch_pieces(own_hidden, back, gain_row, sections)

    pieces = lax.all_to_all(pieces, "section", 0, 0)

    for turn in (2, 1, 3):
        path = [(i, (i + CORES * turn) % lanes) for i in range(lanes)]
        parts[turn] = lax.ppermute(parts[turn], "fsdp", path)
    drift_factor = jnp.einsum("kr,dk->rd", basis_row, drift[0, 0], precision=lax.Precision.HIGH)
    factor = factor_columns(chip, own_keys, other_keys, drift_factor, parts)
    rank_share = momentum.shape[1]
    island = lax.axis_index("island")

    def rows_of(flip):
        at = jnp.bitwise_xor(island, flip) * rank_share
        return lax.dynamic_slice_in_dim(factor, at, rank_share, 0)

    def exchange(rows, flip):
        path = [(i, i ^ flip) for i in range(islands)]
        return lax.ppermute(rows.astype(jnp.bfloat16), "island", path).astype(jnp.float32)

    rows = exchange(jnp.concatenate([rows_of(1), rows_of(2)]), 1)
    own_sum = rows_of(0) + rows[:rank_share]
    other_sum = rows_of(3) + rows[rank_share:]
    sums, own_sum, other_sum = lax.optimization_barrier((suffix_sums(pieces), own_sum, other_sum))
    pieces = lax.all_to_all(sums, "section", 0, 0)
    input_grad = pieces.reshape(tokens, width)

    mean_weight = (1.0 + momentum_rate) / islands
    ride = momentum_rate * momentum_rate / mean_weight
    pair_sums = jnp.stack([own_sum + ride * momentum[0], other_sum]).astype(jnp.bfloat16)
    pair_sums = lax.all_gather(pair_sums, "island")
    other_pair = lax.dynamic_index_in_dim(pair_sums, jnp.bitwise_xor(island, 3), 0, False)[1]
    own_mean = (own_sum + other_pair.astype(jnp.float32)) / islands
    own_momentum = momentum_rate * momentum[0] + own_mean
    pair_sums = pair_sums.astype(jnp.float32)
    total = jnp.concatenate([pair_sums[i, 0] + pair_sums[i ^ 3, 1] for i in range(islands)])
    outer_update = (outer_rate * mean_weight) * jnp.einsum(
        "rd,kr->dk", total, basis_row, precision=lax.Precision.HIGH
    )
    return (input_grad[None, None], own_momentum[None], outer_update[None])


def solution(mesh):
    return jax.shard_map(
        shards,
        mesh=mesh,
        in_specs=(
            P("island", "section", "fsdp", None),
            P("section", None),
            P("island", "section", "fsdp", None),
            P("island", "section", "fsdp", None),
            P("island", "section", "fsdp", None),
            P("section", "island", "fsdp"),
            P("section"),
        ),
        out_specs=(
            P("island", "section", "fsdp", None),
            P("section", "island", "fsdp"),
            P("section", "fsdp", None),
        ),
        check_vma=False,
    )
```

```python
import math

import jax
import jax.numpy as jnp
from jax import lax
from jax.experimental import pallas as pl
from jax.experimental.pallas import tpu as pltpu
from jax.sharding import PartitionSpec as P

RANK = 256
CORES = 2


inner_rate = 0.01
outer_rate = 0.7
momentum_rate = 0.9


def projection_basis(seed_value, row_count, column_count):
    row_index = lax.broadcasted_iota(jnp.int32, (row_count, column_count), 0)
    column_index = lax.broadcasted_iota(jnp.int32, (row_count, column_count), 1)
    hashed = row_index * column_count + column_index + seed_value * 7919
    hashed = hashed * 1664525 + 1013904223 & 2147483647
    hashed = hashed ^ hashed >> 15
    hashed = hashed * 1103515245 + 12345 & 2147483647
    hashed = hashed ^ hashed >> 13
    levels = (hashed & 65535).astype(jnp.float32)
    return (levels - 32767.5) * (math.sqrt(12.0 / column_count) / 65536.0)


def whole_vmem():
    return pl.BlockSpec(memory_space=pltpu.VMEM)


def whole_hbm():
    return pl.BlockSpec(memory_space=pltpu.HBM)


def anywhere():
    return pl.BlockSpec(memory_space=pl.ANY)


def in_vmem(array):
    return pltpu.with_memory_space_constraint(array, pltpu.VMEM)


def in_hbm(array):
    return pltpu.with_memory_space_constraint(array, pltpu.HBM)


def kernel_params():
    return pltpu.CompilerParams(vmem_limit_bytes=8 * 1024 * 1024)


def suffix_kernel(parts_ref, sums_ref, out, out_sems):
    chunks, count, _, step = out.shape

    def departure(place):
        span = pl.ds(place * step, step)
        return pltpu.make_async_copy(out.at[place], sums_ref.at[:, :, span], out_sems.at[place])

    for place in range(chunks):
        span = pl.ds(place * step, step)
        total = parts_ref[count - 1, :, span].astype(jnp.float32)
        out[place, count - 1] = total.astype(out.dtype)
        for source in range(count - 2, -1, -1):
            total = total + parts_ref[source, :, span].astype(jnp.float32)
            out[place, source] = total.astype(out.dtype)
        departure(place).start()
    for place in range(chunks):
        departure(place).wait()


def suffix_sums(parts):
    count, rows, width = parts.shape
    step = 512
    chunks = width // step
    return pl.pallas_call(
        suffix_kernel,
        out_shape=pltpu.HBM(parts.shape, parts.dtype),
        in_specs=[whole_vmem()],
        out_specs=whole_hbm(),
        scratch_shapes=[
            pltpu.VMEM((chunks, count, rows, step), parts.dtype),
            pltpu.SemaphoreType.DMA((chunks,)),
        ],
        compiler_params=kernel_params(),
        name="suffix_sums",
    )(pltpu.with_memory_space_constraint(parts, pltpu.VMEM))


def key_back_kernel(core_ref, keys_ref, own_ref, other_ref, back_ref, out, out_sems):
    chips, tokens, depth = keys_ref.shape
    width = own_ref.shape[0]
    core = core_ref[0]
    keys = keys_ref[...].reshape(chips * tokens, depth)

    def departure(side, chip):
        span = pl.ds(pl.multiple_of((core if side == 0 else 1 - core) * width, width), width)
        return pltpu.make_async_copy(
            out.at[side, chip], back_ref.at[chip, :, span], out_sems.at[side, chip]
        )

    for side, weight_ref in enumerate((own_ref, other_ref)):
        product = lax.dot_general(
            keys,
            weight_ref[0:width, :],
            (((1,), (1,)), ((), ())),
            preferred_element_type=jnp.float32,
        ).astype(out.dtype)
        for chip in range(chips):
            out[side, chip] = product[chip * tokens : (chip + 1) * tokens]
            departure(side, chip).start()
    for side in range(CORES):
        for chip in range(chips):
            departure(side, chip).wait()


def key_back_columns(core, keys, own_weight, arrived):
    chips, tokens, _ = keys.shape
    width = own_weight.shape[0]
    return pl.pallas_call(
        key_back_kernel,
        out_shape=pltpu.HBM((chips, tokens, CORES * width), jnp.bfloat16),
        in_specs=[pl.BlockSpec(memory_space=pltpu.SMEM)] + [whole_vmem()] * 3,
        out_specs=whole_hbm(),
        scratch_shapes=[
            pltpu.VMEM((CORES, chips, tokens, width), jnp.bfloat16),
            pltpu.SemaphoreType.DMA((CORES, chips)),
        ],
        compiler_params=kernel_params(),
        name="key_back_columns",
    )(core.reshape(1), keys, own_weight, arrived)


def prepare_kernel(
    core_ref, hidden_ref, gain_ref, weight_ref, own_ref, swap_ref, held, gain, out, held_sems, out_sems
):
    tokens, width = hidden_ref.shape
    chips, _, slice_width = own_ref.shape
    chunks = held_sems.shape[0] - 2
    rows = tokens // chunks
    core = core_ref[0]

    def arrival(chunk):
        lines = pl.ds(chunk * rows, rows)
        return pltpu.make_async_copy(hidden_ref.at[lines], held.at[lines], held_sems.at[chunk])

    def departure(chunk):
        lines = pl.ds(chunk * rows, rows)
        return pltpu.make_async_copy(out.at[:, lines], own_ref.at[:, lines], out_sems.at[chunk])

    gain_in = pltpu.make_async_copy(gain_ref, gain, held_sems.at[chunks])
    weight_in = pltpu.make_async_copy(
        weight_ref, swap_ref.at[pl.ds(0, chips)], held_sems.at[chunks + 1]
    )
    arrival(0).start()
    gain_in.start()
    for chunk in range(1, chunks):
        arrival(chunk).start()
    weight_in.start()
    for chunk in range(chunks):
        arrival(chunk).wait()
        lines = pl.ds(chunk * rows, rows)
        squares = [jnp.zeros((rows, 128), jnp.float32)] * 2
        for column in range(width // 128):
            value = held[lines, column * 128 : column * 128 + 128].astype(jnp.float32)
            squares[column % 2] = squares[column % 2] + value * value
        total = jnp.sum(squares[0] + squares[1], -1, keepdims=True)
        recip = lax.rsqrt(total / width + 1e-05)
        if chunk == 0:
            gain_in.wait()
        for chip in range(chips):
            for to_ref, at, place in ((out, chip, core), (swap_ref, chips + chip, 1 - core)):
                first = pl.multiple_of((CORES * chip + place) * slice_width, slice_width)
                for column in range(0, slice_width, 128):
                    span = pl.ds(pl.multiple_of(first + column, 128), 128)
                    value = held[lines, span].astype(jnp.float32) * recip
                    normed = (value * gain[:, span]).astype(to_ref.dtype)
                    to_ref[at, lines, column : column + 128] = normed
        departure(chunk).start()
    weight_in.wait()
    for chunk in range(chunks):
        departure(chunk).wait()


def prepare(core, hidden, gain_row, weight):
    tokens, width = hidden.shape
    slice_width, key_width = weight.shape
    chips = width // slice_width // CORES
    chunks = 2
    own, swapped = pl.pallas_call(
        prepare_kernel,
        out_shape=(
            pltpu.HBM((chips, tokens, slice_width), jnp.bfloat16),
            pltpu.VMEM((2 * chips, tokens, slice_width), jnp.bfloat16),
        ),
        in_specs=[pl.BlockSpec(memory_space=pltpu.SMEM)] + [whole_hbm()] * 3,
        out_specs=(whole_hbm(), whole_vmem()),
        scratch_shapes=[
            pltpu.VMEM(hidden.shape, hidden.dtype),
            pltpu.VMEM(gain_row.shape, gain_row.dtype),
            pltpu.VMEM((chips, tokens, slice_width), jnp.bfloat16),
            pltpu.SemaphoreType.DMA((chunks + 2,)),
            pltpu.SemaphoreType.DMA((chunks,)),
        ],
        compiler_params=kernel_params(),
        name="prepare",
    )(
        core.reshape(1),
        in_hbm(hidden),
        in_hbm(gain_row),
        in_hbm(weight.reshape(chips, tokens, key_width)),
    )
    return own, swapped.reshape(2 * chips * tokens, slice_width)


def pair_kernel(chip_ref, own_ref, other_ref, *refs):
    part_refs, (held, in_sems, out_sems) = refs[:-3], refs[-3:]
    chips, tokens, _ = own_ref.shape
    first = other_ref.shape[0] - chips * tokens
    arrivals, departures = [], []
    for turn, part_ref in enumerate(part_refs):
        target = lax.rem(chip_ref[0] + turn, chips)
        lines = pl.ds(pl.multiple_of(first + target * tokens, tokens), tokens)
        for side, source in enumerate((own_ref.at[target], other_ref.at[lines])):
            place = held.at[turn, side]
            arrivals.append(pltpu.make_async_copy(source, place, in_sems.at[turn, side]))
            departures.append(
                pltpu.make_async_copy(place, part_ref.at[side], out_sems.at[turn, side])
            )
    for copy in arrivals:
        copy.start()
    for arrival, departure in zip(arrivals, departures, strict=True):
        arrival.wait()
        departure.start()
    for copy in departures:
        copy.wait()


def pair_columns(chip, own_normed, arrived):
    chips, tokens, slice_width = own_normed.shape
    shape = (CORES, tokens, slice_width)
    return pl.pallas_call(
        pair_kernel,
        out_shape=(pltpu.HBM(shape, own_normed.dtype),) * chips,
        in_specs=[pl.BlockSpec(memory_space=pltpu.SMEM), anywhere(), anywhere()],
        out_specs=(whole_hbm(),) * chips,
        scratch_shapes=[
            pltpu.VMEM((chips, *shape), own_normed.dtype),
            pltpu.SemaphoreType.DMA((chips, CORES)),
            pltpu.SemaphoreType.DMA((chips, CORES)),
        ],
        compiler_params=kernel_params(),
        name="pair_columns",
    )(chip.reshape(1), own_normed, arrived)


def factor_kernel(chip_ref, own_keys, other_keys, drift_ref, part0, part1, part2, part3, sum_ref):
    chips = own_keys.shape[0]
    total = jnp.zeros(sum_ref.shape, jnp.float32)
    for turn, part_ref in enumerate((part0, part1, part2, part3)):
        source = lax.rem(chip_ref[0] + (chips - turn), chips)
        for side, keys_ref in enumerate((own_keys, other_keys)):
            total = total + lax.dot_general(
                keys_ref[source],
                part_ref[side],
                (((0,), (0,)), ((), ())),
                preferred_element_type=jnp.float32,
            )
    sum_ref[...] = drift_ref[...] + inner_rate * total


def factor_columns(chip, own_keys, other_keys, drift_factor, parts):
    return pl.pallas_call(
        factor_kernel,
        out_shape=jax.ShapeDtypeStruct(drift_factor.shape, jnp.float32),
        in_specs=[pl.BlockSpec(memory_space=pltpu.SMEM)] + [whole_vmem()] * 7,
        out_specs=whole_vmem(),
        compiler_params=kernel_params(),
        name="factor_columns",
    )(chip.reshape(1), own_keys, other_keys, drift_factor, *parts)


def branch_kernel(hidden_ref, back_ref, gain_ref, pieces_ref, out, out_sem):
    tokens, width = hidden_ref.shape
    chips, _, span = back_ref.shape
    rows = 16
    count = pieces_ref.shape[1]
    each = rows // count
    columns = [(chip, column) for chip in range(chips) for column in range(0, span, 128)]

    def departure(place):
        run = pl.ds(place * each, each)
        return pltpu.make_async_copy(out.at[run], pieces_ref.at[run], out_sem)

    for place in range(tokens // rows):
        lines = pl.ds(place * rows, rows)

        def tile(chip, column, lines=lines):
            at = chip * span + column
            value = hidden_ref[lines, at : at + 128].astype(jnp.float32)
            back = back_ref[chip, lines, column : column + 128].astype(jnp.float32)
            return at, value, back * gain_ref[:, at : at + 128]

        squares = [jnp.zeros((rows, 128), jnp.float32)] * 2
        cross = [jnp.zeros((rows, 128), jnp.float32)] * 2
        for index, (chip, column) in enumerate(columns):
            _, value, scaled = tile(chip, column)
            squares[index % 2] = squares[index % 2] + value * value
            cross[index % 2] = cross[index % 2] + value * scaled
        total = jnp.sum(squares[0] + squares[1], -1, keepdims=True)
        recip = lax.rsqrt(total / width + 1e-05)
        mean = jnp.sum(cross[0] + cross[1], -1, keepdims=True) * recip / width
        share = recip * recip * mean
        for chip, column in columns:
            at, value, scaled = tile(chip, column)
            branch = (recip * scaled - share * value).astype(out.dtype)
            for part in range(each):
                lines_of = branch[part * count : (part + 1) * count]
                out[place * each + part, :, at : at + 128] = lines_of
        departure(place).start()
    pltpu.make_async_copy(out, pieces_ref, out_sem).wait()


def branch_pieces(hidden, back, gain_row, sections):
    tokens, width = hidden.shape
    shape = (sections, tokens // sections, width)
    return pl.pallas_call(
        branch_kernel,
        out_shape=pltpu.HBM(shape, jnp.bfloat16),
        in_specs=[whole_vmem()] * 3,
        out_specs=whole_hbm(),
        scratch_shapes=[pltpu.VMEM(shape, jnp.bfloat16), pltpu.SemaphoreType.DMA],
        compiler_params=kernel_params(),
        name="branch_pieces",
    )(pltpu.with_memory_space_constraint(hidden, pltpu.VMEM), back, gain_row)


def shards(hidden, norm_gain, key_grad, local_weight, drift, momentum, seeds):
    tokens, width = hidden.shape[2:]
    sections = lax.axis_size("section")
    islands = lax.axis_size("island")
    lanes = lax.axis_size("fsdp")
    chips = lanes // CORES
    lane = lax.axis_index("fsdp")
    chip, core = lane // CORES, lane - lane // CORES * CORES
    swap = [(i, i ^ 1) for i in range(lanes)]
    x_lines = [[c + CORES * i for i in range(chips)] for c in range(CORES)]
    gain_row = norm_gain
    own_hidden = hidden[0, 0]
    own_weight = local_weight[0, 0]
    slice_width = own_weight.shape[0]
    span = CORES * slice_width

    own_normed, swapped = prepare(core, own_hidden, gain_row, own_weight)
    swapped, sent_keys = lax.optimization_barrier((swapped, key_grad[0, 0]))
    arrived = lax.ppermute(swapped, "fsdp", swap)
    line_keys = lax.all_gather(sent_keys, "fsdp", axis_index_groups=x_lines)
    back = key_back_columns(core, line_keys, own_weight, arrived)
    back, own_normed, arrived = lax.optimization_barrier((back, own_normed, arrived))
    back = lax.all_to_all(back, "fsdp", 0, 0, axis_index_groups=x_lines)
    parts = list(pair_columns(chip, own_normed, arrived))
    basis_row = projection_basis(seeds[0], line_keys.shape[2], RANK)
    own_keys = lax.dot_general(
        line_keys,
        basis_row.astype(jnp.bfloat16),
        (((2,), (0,)), ((), ())),
        preferred_element_type=jnp.float32,
    ).astype(jnp.bfloat16)
    other_keys = lax.ppermute(own_keys, "fsdp", swap)
    back, own_keys, other_keys, *parts = lax.optimization_barrier(
        (back, own_keys, other_keys, *parts)
    )
    pieces = branch_pieces(own_hidden, back, gain_row, sections)

    pieces = lax.all_to_all(pieces, "section", 0, 0)

    for turn in (2, 1, 3):
        path = [(i, (i + CORES * turn) % lanes) for i in range(lanes)]
        parts[turn] = lax.ppermute(parts[turn], "fsdp", path)
    drift_factor = jnp.einsum("kr,dk->rd", basis_row, drift[0, 0], precision=lax.Precision.HIGH)
    factor = factor_columns(chip, own_keys, other_keys, drift_factor, parts)
    rank_share = momentum.shape[1]
    island = lax.axis_index("island")

    def rows_of(flip):
        at = jnp.bitwise_xor(island, flip) * rank_share
        return lax.dynamic_slice_in_dim(factor, at, rank_share, 0)

    def exchange(rows, flip):
        path = [(i, i ^ flip) for i in range(islands)]
        return lax.ppermute(rows.astype(jnp.bfloat16), "island", path).astype(jnp.float32)

    rows = exchange(jnp.concatenate([rows_of(1), rows_of(2)]), 1)
    own_sum = rows_of(0) + rows[:rank_share]
    other_sum = rows_of(3) + rows[rank_share:]
    sums, own_sum, other_sum = lax.optimization_barrier((suffix_sums(pieces), own_sum, other_sum))
    pieces = lax.all_to_all(sums, "section", 0, 0)
    input_grad = pieces.reshape(tokens, width)

    mean_weight = (1.0 + momentum_rate) / islands
    ride = momentum_rate * momentum_rate / mean_weight
    pair_sums = jnp.stack([own_sum + ride * momentum[0], other_sum]).astype(jnp.bfloat16)
    pair_sums = lax.all_gather(pair_sums, "island")
    other_pair = lax.dynamic_index_in_dim(pair_sums, jnp.bitwise_xor(island, 3), 0, False)[1]
    own_mean = (own_sum + other_pair.astype(jnp.float32)) / islands
    own_momentum = momentum_rate * momentum[0] + own_mean
    pair_sums = pair_sums.astype(jnp.float32)
    total = jnp.concatenate([pair_sums[i, 0] + pair_sums[i ^ 3, 1] for i in range(islands)])
    outer_update = (outer_rate * mean_weight) * jnp.einsum(
        "rd,kr->dk", total, basis_row, precision=lax.Precision.HIGH
    )
    return (input_grad[None, None], own_momentum[None], outer_update[None])


def solution(mesh):
    return jax.shard_map(
        shards,
        mesh=mesh,
        in_specs=(
            P("island", "section", "fsdp", None),
            P("section", None),
            P("island", "section", "fsdp", None),
            P("island", "section", "fsdp", None),
            P("island", "section", "fsdp", None),
            P("section", "island", "fsdp"),
            P("section"),
        ),
        out_specs=(
            P("island", "section", "fsdp", None),
            P("section", "island", "fsdp"),
            P("section", "fsdp", None),
        ),
        check_vma=False,
    )
```

```python
import math

import jax
import jax.numpy as jnp
from jax import lax
from jax.experimental import pallas as pl
from jax.experimental.pallas import tpu as pltpu
from jax.sharding import PartitionSpec as P

RANK = 256
CORES = 2


inner_rate = 0.01
outer_rate = 0.7
momentum_rate = 0.9


def projection_basis(seed_value, row_count, column_count):
    row_index = lax.broadcasted_iota(jnp.int32, (row_count, column_count), 0)
    column_index = lax.broadcasted_iota(jnp.int32, (row_count, column_count), 1)
    hashed = row_index * column_count + column_index + seed_value * 7919
    hashed = hashed * 1664525 + 1013904223 & 2147483647
    hashed = hashed ^ hashed >> 15
    hashed = hashed * 1103515245 + 12345 & 2147483647
    hashed = hashed ^ hashed >> 13
    levels = (hashed & 65535).astype(jnp.float32)
    return (levels - 32767.5) * (math.sqrt(12.0 / column_count) / 65536.0)


def whole_vmem():
    return pl.BlockSpec(memory_space=pltpu.VMEM)


def whole_hbm():
    return pl.BlockSpec(memory_space=pltpu.HBM)


def anywhere():
    return pl.BlockSpec(memory_space=pl.ANY)


def in_vmem(array):
    return pltpu.with_memory_space_constraint(array, pltpu.VMEM)


def in_hbm(array):
    return pltpu.with_memory_space_constraint(array, pltpu.HBM)


def kernel_params():
    return pltpu.CompilerParams(vmem_limit_bytes=8 * 1024 * 1024)


def suffix_kernel(parts_ref, sums_ref, out, out_sems):
    chunks, count, _, step = out.shape

    def departure(place):
        span = pl.ds(place * step, step)
        return pltpu.make_async_copy(out.at[place], sums_ref.at[:, :, span], out_sems.at[place])

    for place in range(chunks):
        span = pl.ds(place * step, step)
        total = parts_ref[count - 1, :, span].astype(jnp.float32)
        out[place, count - 1] = total.astype(out.dtype)
        for source in range(count - 2, -1, -1):
            total = total + parts_ref[source, :, span].astype(jnp.float32)
            out[place, source] = total.astype(out.dtype)
        departure(place).start()
    for place in range(chunks):
        departure(place).wait()


def suffix_sums(parts):
    count, rows, width = parts.shape
    step = 512
    chunks = width // step
    return pl.pallas_call(
        suffix_kernel,
        out_shape=pltpu.HBM(parts.shape, parts.dtype),
        in_specs=[whole_vmem()],
        out_specs=whole_hbm(),
        scratch_shapes=[
            pltpu.VMEM((chunks, count, rows, step), parts.dtype),
            pltpu.SemaphoreType.DMA((chunks,)),
        ],
        compiler_params=kernel_params(),
        name="suffix_sums",
    )(pltpu.with_memory_space_constraint(parts, pltpu.VMEM))


def key_back_kernel(core_ref, keys_ref, own_ref, other_ref, back_ref, out, out_sems):
    chips, tokens, depth = keys_ref.shape
    width = own_ref.shape[0]
    core = core_ref[0]
    keys = keys_ref[...].reshape(chips * tokens, depth)

    def departure(side, chip):
        span = pl.ds(pl.multiple_of((core if side == 0 else 1 - core) * width, width), width)
        return pltpu.make_async_copy(
            out.at[side, chip], back_ref.at[chip, :, span], out_sems.at[side, chip]
        )

    for side, weight_ref in enumerate((own_ref, other_ref)):
        product = lax.dot_general(
            keys,
            weight_ref[0:width, :],
            (((1,), (1,)), ((), ())),
            preferred_element_type=jnp.float32,
        ).astype(out.dtype)
        for chip in range(chips):
            out[side, chip] = product[chip * tokens : (chip + 1) * tokens]
            departure(side, chip).start()
    for side in range(CORES):
        for chip in range(chips):
            departure(side, chip).wait()


def key_back_columns(core, keys, own_weight, arrived):
    chips, tokens, _ = keys.shape
    width = own_weight.shape[0]
    return pl.pallas_call(
        key_back_kernel,
        out_shape=pltpu.HBM((chips, tokens, CORES * width), jnp.bfloat16),
        in_specs=[pl.BlockSpec(memory_space=pltpu.SMEM)] + [whole_vmem()] * 3,
        out_specs=whole_hbm(),
        scratch_shapes=[
            pltpu.VMEM((CORES, chips, tokens, width), jnp.bfloat16),
            pltpu.SemaphoreType.DMA((CORES, chips)),
        ],
        compiler_params=kernel_params(),
        name="key_back_columns",
    )(core.reshape(1), keys, own_weight, arrived)


def prepare_kernel(
    core_ref, hidden_ref, gain_ref, weight_ref, own_ref, swap_ref, held, gain, out, held_sems, out_sems
):
    tokens, width = hidden_ref.shape
    chips, _, slice_width = own_ref.shape
    chunks = held_sems.shape[0] - 2
    rows = tokens // chunks
    core = core_ref[0]

    def arrival(chunk):
        lines = pl.ds(chunk * rows, rows)
        return pltpu.make_async_copy(hidden_ref.at[lines], held.at[lines], held_sems.at[chunk])

    def departure(chunk):
        lines = pl.ds(chunk * rows, rows)
        return pltpu.make_async_copy(out.at[:, lines], own_ref.at[:, lines], out_sems.at[chunk])

    gain_in = pltpu.make_async_copy(gain_ref, gain, held_sems.at[chunks])
    weight_in = pltpu.make_async_copy(
        weight_ref, swap_ref.at[pl.ds(0, chips)], held_sems.at[chunks + 1]
    )
    arrival(0).start()
    gain_in.start()
    for chunk in range(1, chunks):
        arrival(chunk).start()
    weight_in.start()
    for chunk in range(chunks):
        arrival(chunk).wait()
        lines = pl.ds(chunk * rows, rows)
        squares = [jnp.zeros((rows, 128), jnp.float32)] * 2
        for column in range(width // 128):
            value = held[lines, column * 128 : column * 128 + 128].astype(jnp.float32)
            squares[column % 2] = squares[column % 2] + value * value
        total = jnp.sum(squares[0] + squares[1], -1, keepdims=True)
        recip = lax.rsqrt(total / width + 1e-05)
        if chunk == 0:
            gain_in.wait()
        for chip in range(chips):
            for to_ref, at, place in ((out, chip, core), (swap_ref, chips + chip, 1 - core)):
                first = pl.multiple_of((CORES * chip + place) * slice_width, slice_width)
                for column in range(0, slice_width, 128):
                    span = pl.ds(pl.multiple_of(first + column, 128), 128)
                    value = held[lines, span].astype(jnp.float32) * recip
                    normed = (value * gain[:, span]).astype(to_ref.dtype)
                    to_ref[at, lines, column : column + 128] = normed
        departure(chunk).start()
    weight_in.wait()
    for chunk in range(chunks):
        departure(chunk).wait()


def prepare(core, hidden, gain_row, weight):
    tokens, width = hidden.shape
    slice_width, key_width = weight.shape
    chips = width // slice_width // CORES
    chunks = 2
    own, swapped = pl.pallas_call(
        prepare_kernel,
        out_shape=(
            pltpu.HBM((chips, tokens, slice_width), jnp.bfloat16),
            pltpu.VMEM((2 * chips, tokens, slice_width), jnp.bfloat16),
        ),
        in_specs=[pl.BlockSpec(memory_space=pltpu.SMEM)] + [whole_hbm()] * 3,
        out_specs=(whole_hbm(), whole_vmem()),
        scratch_shapes=[
            pltpu.VMEM(hidden.shape, hidden.dtype),
            pltpu.VMEM(gain_row.shape, gain_row.dtype),
            pltpu.VMEM((chips, tokens, slice_width), jnp.bfloat16),
            pltpu.SemaphoreType.DMA((chunks + 2,)),
            pltpu.SemaphoreType.DMA((chunks,)),
        ],
        compiler_params=kernel_params(),
        name="prepare",
    )(
        core.reshape(1),
        in_hbm(hidden),
        in_hbm(gain_row),
        in_hbm(weight.reshape(chips, tokens, key_width)),
    )
    return own, swapped.reshape(2 * chips * tokens, slice_width)


def pair_kernel(chip_ref, own_ref, other_ref, *refs):
    part_refs, (held, in_sems, out_sems) = refs[:-3], refs[-3:]
    chips, tokens, _ = own_ref.shape
    first = other_ref.shape[0] - chips * tokens
    arrivals, departures = [], []
    for turn, part_ref in enumerate(part_refs):
        target = lax.rem(chip_ref[0] + turn, chips)
        lines = pl.ds(pl.multiple_of(first + target * tokens, tokens), tokens)
        for side, source in enumerate((own_ref.at[target], other_ref.at[lines])):
            place = held.at[turn, side]
            arrivals.append(pltpu.make_async_copy(source, place, in_sems.at[turn, side]))
            departures.append(
                pltpu.make_async_copy(place, part_ref.at[side], out_sems.at[turn, side])
            )
    for copy in arrivals:
        copy.start()
    for arrival, departure in zip(arrivals, departures, strict=True):
        arrival.wait()
        departure.start()
    for copy in departures:
        copy.wait()


def pair_columns(chip, own_normed, arrived):
    chips, tokens, slice_width = own_normed.shape
    shape = (CORES, tokens, slice_width)
    return pl.pallas_call(
        pair_kernel,
        out_shape=(pltpu.HBM(shape, own_normed.dtype),) * chips,
        in_specs=[pl.BlockSpec(memory_space=pltpu.SMEM), anywhere(), anywhere()],
        out_specs=(whole_hbm(),) * chips,
        scratch_shapes=[
            pltpu.VMEM((chips, *shape), own_normed.dtype),
            pltpu.SemaphoreType.DMA((chips, CORES)),
            pltpu.SemaphoreType.DMA((chips, CORES)),
        ],
        compiler_params=kernel_params(),
        name="pair_columns",
    )(chip.reshape(1), own_normed, arrived)


def factor_kernel(chip_ref, own_keys, other_keys, drift_ref, part0, part1, part2, part3, sum_ref):
    chips = own_keys.shape[0]
    total = jnp.zeros(sum_ref.shape, jnp.float32)
    for turn, part_ref in enumerate((part0, part1, part2, part3)):
        source = lax.rem(chip_ref[0] + (chips - turn), chips)
        for side, keys_ref in enumerate((own_keys, other_keys)):
            total = total + lax.dot_general(
                keys_ref[source],
                part_ref[side],
                (((0,), (0,)), ((), ())),
                preferred_element_type=jnp.float32,
            )
    sum_ref[...] = drift_ref[...] + inner_rate * total


def factor_columns(chip, own_keys, other_keys, drift_factor, parts):
    return pl.pallas_call(
        factor_kernel,
        out_shape=jax.ShapeDtypeStruct(drift_factor.shape, jnp.float32),
        in_specs=[pl.BlockSpec(memory_space=pltpu.SMEM)] + [whole_vmem()] * 7,
        out_specs=whole_vmem(),
        compiler_params=kernel_params(),
        name="factor_columns",
    )(chip.reshape(1), own_keys, other_keys, drift_factor, *parts)


def branch_kernel(hidden_ref, back_ref, gain_ref, pieces_ref, out, out_sem):
    tokens, width = hidden_ref.shape
    chips, _, span = back_ref.shape
    rows = 16
    count = pieces_ref.shape[1]
    each = rows // count
    columns = [(chip, column) for chip in range(chips) for column in range(0, span, 128)]

    def departure(place):
        run = pl.ds(place * each, each)
        return pltpu.make_async_copy(out.at[run], pieces_ref.at[run], out_sem)

    for place in range(tokens // rows):
        lines = pl.ds(place * rows, rows)

        def tile(chip, column, lines=lines):
            at = chip * span + column
            value = hidden_ref[lines, at : at + 128].astype(jnp.float32)
            back = back_ref[chip, lines, column : column + 128].astype(jnp.float32)
            return at, value, back * gain_ref[:, at : at + 128]

        squares = [jnp.zeros((rows, 128), jnp.float32)] * 2
        cross = [jnp.zeros((rows, 128), jnp.float32)] * 2
        for index, (chip, column) in enumerate(columns):
            _, value, scaled = tile(chip, column)
            squares[index % 2] = squares[index % 2] + value * value
            cross[index % 2] = cross[index % 2] + value * scaled
        total = jnp.sum(squares[0] + squares[1], -1, keepdims=True)
        recip = lax.rsqrt(total / width + 1e-05)
        mean = jnp.sum(cross[0] + cross[1], -1, keepdims=True) * recip / width
        share = recip * recip * mean
        for chip, column in columns:
            at, value, scaled = tile(chip, column)
            branch = (recip * scaled - share * value).astype(out.dtype)
            for part in range(each):
                lines_of = branch[part * count : (part + 1) * count]
                out[place * each + part, :, at : at + 128] = lines_of
        departure(place).start()
    pltpu.make_async_copy(out, pieces_ref, out_sem).wait()


def branch_pieces(hidden, back, gain_row, sections):
    tokens, width = hidden.shape
    shape = (sections, tokens // sections, width)
    return pl.pallas_call(
        branch_kernel,
        out_shape=pltpu.HBM(shape, jnp.bfloat16),
        in_specs=[whole_vmem()] * 3,
        out_specs=whole_hbm(),
        scratch_shapes=[pltpu.VMEM(shape, jnp.bfloat16), pltpu.SemaphoreType.DMA],
        compiler_params=kernel_params(),
        name="branch_pieces",
    )(pltpu.with_memory_space_constraint(hidden, pltpu.VMEM), back, gain_row)


def shards(hidden, norm_gain, key_grad, local_weight, drift, momentum, seeds):
    tokens, width = hidden.shape[2:]
    sections = lax.axis_size("section")
    islands = lax.axis_size("island")
    lanes = lax.axis_size("fsdp")
    chips = lanes // CORES
    lane = lax.axis_index("fsdp")
    chip, core = lane // CORES, lane - lane // CORES * CORES
    swap = [(i, i ^ 1) for i in range(lanes)]
    x_lines = [[c + CORES * i for i in range(chips)] for c in range(CORES)]
    gain_row = norm_gain
    own_hidden = hidden[0, 0]
    own_weight = local_weight[0, 0]
    slice_width = own_weight.shape[0]
    span = CORES * slice_width

    own_normed, swapped = prepare(core, own_hidden, gain_row, own_weight)
    swapped, sent_keys = lax.optimization_barrier((swapped, key_grad[0, 0]))
    arrived = lax.ppermute(swapped, "fsdp", swap)
    line_keys = lax.all_gather(sent_keys, "fsdp", axis_index_groups=x_lines)
    back = key_back_columns(core, line_keys, own_weight, arrived)
    back, own_normed, arrived = lax.optimization_barrier((back, own_normed, arrived))
    back = lax.all_to_all(back, "fsdp", 0, 0, axis_index_groups=x_lines)
    parts = list(pair_columns(chip, own_normed, arrived))
    basis_row = projection_basis(seeds[0], line_keys.shape[2], RANK)
    own_keys = lax.dot_general(
        line_keys,
        basis_row.astype(jnp.bfloat16),
        (((2,), (0,)), ((), ())),
        preferred_element_type=jnp.float32,
    ).astype(jnp.bfloat16)
    other_keys = lax.ppermute(own_keys, "fsdp", swap)
    back, own_keys, other_keys, *parts = lax.optimization_barrier(
        (back, own_keys, other_keys, *parts)
    )
    pieces = branch_pieces(own_hidden, back, gain_row, sections)

    pieces = lax.all_to_all(pieces, "section", 0, 0)

    for turn in (2, 1, 3):
        path = [(i, (i + CORES * turn) % lanes) for i in range(lanes)]
        parts[turn] = lax.ppermute(parts[turn], "fsdp", path)
    drift_factor = jnp.einsum("kr,dk->rd", basis_row, drift[0, 0], precision=lax.Precision.HIGH)
    factor = factor_columns(chip, own_keys, other_keys, drift_factor, parts)
    rank_share = momentum.shape[1]
    island = lax.axis_index("island")

    def rows_of(flip):
        at = jnp.bitwise_xor(island, flip) * rank_share
        return lax.dynamic_slice_in_dim(factor, at, rank_share, 0)

    def exchange(rows, flip):
        path = [(i, i ^ flip) for i in range(islands)]
        return lax.ppermute(rows.astype(jnp.bfloat16), "island", path).astype(jnp.float32)

    rows = exchange(jnp.concatenate([rows_of(1), rows_of(2)]), 1)
    own_sum = rows_of(0) + rows[:rank_share]
    other_sum = rows_of(3) + rows[rank_share:]
    sums, own_sum, other_sum, late_basis = lax.optimization_barrier(
        (suffix_sums(pieces), own_sum, other_sum, basis_row)
    )
    pieces = lax.all_to_all(sums, "section", 0, 0)
    input_grad = pieces.reshape(tokens, width)

    mean_weight = (1.0 + momentum_rate) / islands
    ride = momentum_rate * momentum_rate / mean_weight
    pair_sums = jnp.stack([own_sum + ride * momentum[0], other_sum]).astype(jnp.bfloat16)
    pair_sums = lax.all_gather(pair_sums, "island")
    other_pair = lax.dynamic_index_in_dim(pair_sums, jnp.bitwise_xor(island, 3), 0, False)[1]
    own_mean = (own_sum + other_pair.astype(jnp.float32)) / islands
    own_momentum = momentum_rate * momentum[0] + own_mean
    pair_sums = pair_sums.astype(jnp.float32)
    total = jnp.concatenate([pair_sums[i, 0] + pair_sums[i ^ 3, 1] for i in range(islands)])
    outer_update = (outer_rate * mean_weight) * jnp.einsum(
        "rd,kr->dk", total, late_basis, precision=lax.Precision.HIGH
    )
    return (input_grad[None, None], own_momentum[None], outer_update[None])


def solution(mesh):
    return jax.shard_map(
        shards,
        mesh=mesh,
        in_specs=(
            P("island", "section", "fsdp", None),
            P("section", None),
            P("island", "section", "fsdp", None),
            P("island", "section", "fsdp", None),
            P("island", "section", "fsdp", None),
            P("section", "island", "fsdp"),
            P("section"),
        ),
        out_specs=(
            P("island", "section", "fsdp", None),
            P("section", "island", "fsdp"),
            P("section", "fsdp", None),
        ),
        check_vma=False,
    )
```

```python
import math

import jax
import jax.numpy as jnp
from jax import lax
from jax.experimental import pallas as pl
from jax.experimental.pallas import tpu as pltpu
from jax.sharding import PartitionSpec as P

RANK = 256
CORES = 2


inner_rate = 0.01
outer_rate = 0.7
momentum_rate = 0.9


def projection_basis(seed_value, row_count, column_count):
    row_index = lax.broadcasted_iota(jnp.int32, (row_count, column_count), 0)
    column_index = lax.broadcasted_iota(jnp.int32, (row_count, column_count), 1)
    hashed = row_index * column_count + column_index + seed_value * 7919
    hashed = hashed * 1664525 + 1013904223 & 2147483647
    hashed = hashed ^ hashed >> 15
    hashed = hashed * 1103515245 + 12345 & 2147483647
    hashed = hashed ^ hashed >> 13
    levels = (hashed & 65535).astype(jnp.float32)
    return (levels - 32767.5) * (math.sqrt(12.0 / column_count) / 65536.0)


def whole_vmem():
    return pl.BlockSpec(memory_space=pltpu.VMEM)


def whole_hbm():
    return pl.BlockSpec(memory_space=pltpu.HBM)


def anywhere():
    return pl.BlockSpec(memory_space=pl.ANY)


def in_vmem(array):
    return pltpu.with_memory_space_constraint(array, pltpu.VMEM)


def in_hbm(array):
    return pltpu.with_memory_space_constraint(array, pltpu.HBM)


def kernel_params():
    return pltpu.CompilerParams(vmem_limit_bytes=8 * 1024 * 1024)


def suffix_kernel(parts_ref, sums_ref, out, out_sems):
    chunks, count, _, step = out.shape

    def departure(place):
        span = pl.ds(place * step, step)
        return pltpu.make_async_copy(out.at[place], sums_ref.at[:, :, span], out_sems.at[place])

    for place in range(chunks):
        span = pl.ds(place * step, step)
        total = parts_ref[count - 1, :, span].astype(jnp.float32)
        out[place, count - 1] = total.astype(out.dtype)
        for source in range(count - 2, -1, -1):
            total = total + parts_ref[source, :, span].astype(jnp.float32)
            out[place, source] = total.astype(out.dtype)
        departure(place).start()
    for place in range(chunks):
        departure(place).wait()


def suffix_sums(parts):
    count, rows, width = parts.shape
    step = 1024
    chunks = width // step
    return pl.pallas_call(
        suffix_kernel,
        out_shape=pltpu.HBM(parts.shape, parts.dtype),
        in_specs=[whole_vmem()],
        out_specs=whole_hbm(),
        scratch_shapes=[
            pltpu.VMEM((chunks, count, rows, step), parts.dtype),
            pltpu.SemaphoreType.DMA((chunks,)),
        ],
        compiler_params=kernel_params(),
        name="suffix_sums",
    )(pltpu.with_memory_space_constraint(parts, pltpu.VMEM))


def key_back_kernel(core_ref, keys_ref, own_ref, other_ref, back_ref, out, out_sems):
    chips, tokens, depth = keys_ref.shape
    width = own_ref.shape[0]
    core = core_ref[0]
    keys = keys_ref[...].reshape(chips * tokens, depth)

    def departure(side, chip):
        span = pl.ds(pl.multiple_of((core if side == 0 else 1 - core) * width, width), width)
        return pltpu.make_async_copy(
            out.at[side, chip], back_ref.at[chip, :, span], out_sems.at[side, chip]
        )

    for side, weight_ref in enumerate((own_ref, other_ref)):
        product = lax.dot_general(
            keys,
            weight_ref[0:width, :],
            (((1,), (1,)), ((), ())),
            preferred_element_type=jnp.float32,
        ).astype(out.dtype)
        for chip in range(chips):
            out[side, chip] = product[chip * tokens : (chip + 1) * tokens]
            departure(side, chip).start()
    for side in range(CORES):
        for chip in range(chips):
            departure(side, chip).wait()


def key_back_columns(core, keys, own_weight, arrived):
    chips, tokens, _ = keys.shape
    width = own_weight.shape[0]
    return pl.pallas_call(
        key_back_kernel,
        out_shape=pltpu.HBM((chips, tokens, CORES * width), jnp.bfloat16),
        in_specs=[pl.BlockSpec(memory_space=pltpu.SMEM)] + [whole_vmem()] * 3,
        out_specs=whole_hbm(),
        scratch_shapes=[
            pltpu.VMEM((CORES, chips, tokens, width), jnp.bfloat16),
            pltpu.SemaphoreType.DMA((CORES, chips)),
        ],
        compiler_params=kernel_params(),
        name="key_back_columns",
    )(core.reshape(1), keys, own_weight, arrived)


def prepare_kernel(
    core_ref, hidden_ref, gain_ref, weight_ref, own_ref, swap_ref, held, gain, out, held_sems, out_sems
):
    tokens, width = hidden_ref.shape
    chips, _, slice_width = own_ref.shape
    chunks = held_sems.shape[0] - 2
    rows = tokens // chunks
    core = core_ref[0]

    def arrival(chunk):
        lines = pl.ds(chunk * rows, rows)
        return pltpu.make_async_copy(hidden_ref.at[lines], held.at[lines], held_sems.at[chunk])

    def departure(chunk):
        lines = pl.ds(chunk * rows, rows)
        return pltpu.make_async_copy(out.at[:, lines], own_ref.at[:, lines], out_sems.at[chunk])

    gain_in = pltpu.make_async_copy(gain_ref, gain, held_sems.at[chunks])
    weight_in = pltpu.make_async_copy(
        weight_ref, swap_ref.at[pl.ds(0, chips)], held_sems.at[chunks + 1]
    )
    arrival(0).start()
    gain_in.start()
    for chunk in range(1, chunks):
        arrival(chunk).start()
    weight_in.start()
    for chunk in range(chunks):
        arrival(chunk).wait()
        lines = pl.ds(chunk * rows, rows)
        squares = [jnp.zeros((rows, 128), jnp.float32)] * 2
        for column in range(width // 128):
            value = held[lines, column * 128 : column * 128 + 128].astype(jnp.float32)
            squares[column % 2] = squares[column % 2] + value * value
        total = jnp.sum(squares[0] + squares[1], -1, keepdims=True)
        recip = lax.rsqrt(total / width + 1e-05)
        if chunk == 0:
            gain_in.wait()
        for chip in range(chips):
            for to_ref, at, place in ((out, chip, core), (swap_ref, chips + chip, 1 - core)):
                first = pl.multiple_of((CORES * chip + place) * slice_width, slice_width)
                for column in range(0, slice_width, 128):
                    span = pl.ds(pl.multiple_of(first + column, 128), 128)
                    value = held[lines, span].astype(jnp.float32) * recip
                    normed = (value * gain[:, span]).astype(to_ref.dtype)
                    to_ref[at, lines, column : column + 128] = normed
        departure(chunk).start()
    weight_in.wait()
    for chunk in range(chunks):
        departure(chunk).wait()


def prepare(core, hidden, gain_row, weight):
    tokens, width = hidden.shape
    slice_width, key_width = weight.shape
    chips = width // slice_width // CORES
    chunks = 2
    own, swapped = pl.pallas_call(
        prepare_kernel,
        out_shape=(
            pltpu.HBM((chips, tokens, slice_width), jnp.bfloat16),
            pltpu.VMEM((2 * chips, tokens, slice_width), jnp.bfloat16),
        ),
        in_specs=[pl.BlockSpec(memory_space=pltpu.SMEM)] + [whole_hbm()] * 3,
        out_specs=(whole_hbm(), whole_vmem()),
        scratch_shapes=[
            pltpu.VMEM(hidden.shape, hidden.dtype),
            pltpu.VMEM(gain_row.shape, gain_row.dtype),
            pltpu.VMEM((chips, tokens, slice_width), jnp.bfloat16),
            pltpu.SemaphoreType.DMA((chunks + 2,)),
            pltpu.SemaphoreType.DMA((chunks,)),
        ],
        compiler_params=kernel_params(),
        name="prepare",
    )(
        core.reshape(1),
        in_hbm(hidden),
        in_hbm(gain_row),
        in_hbm(weight.reshape(chips, tokens, key_width)),
    )
    return own, swapped.reshape(2 * chips * tokens, slice_width)


def pair_kernel(chip_ref, own_ref, other_ref, *refs):
    part_refs, (held, in_sems, out_sems) = refs[:-3], refs[-3:]
    chips, tokens, _ = own_ref.shape
    first = other_ref.shape[0] - chips * tokens
    arrivals, departures = [], []
    for turn, part_ref in enumerate(part_refs):
        target = lax.rem(chip_ref[0] + turn, chips)
        lines = pl.ds(pl.multiple_of(first + target * tokens, tokens), tokens)
        for side, source in enumerate((own_ref.at[target], other_ref.at[lines])):
            place = held.at[turn, side]
            arrivals.append(pltpu.make_async_copy(source, place, in_sems.at[turn, side]))
            departures.append(
                pltpu.make_async_copy(place, part_ref.at[side], out_sems.at[turn, side])
            )
    for copy in arrivals:
        copy.start()
    for arrival, departure in zip(arrivals, departures, strict=True):
        arrival.wait()
        departure.start()
    for copy in departures:
        copy.wait()


def pair_columns(chip, own_normed, arrived):
    chips, tokens, slice_width = own_normed.shape
    shape = (CORES, tokens, slice_width)
    return pl.pallas_call(
        pair_kernel,
        out_shape=(pltpu.HBM(shape, own_normed.dtype),) * chips,
        in_specs=[pl.BlockSpec(memory_space=pltpu.SMEM), anywhere(), anywhere()],
        out_specs=(whole_hbm(),) * chips,
        scratch_shapes=[
            pltpu.VMEM((chips, *shape), own_normed.dtype),
            pltpu.SemaphoreType.DMA((chips, CORES)),
            pltpu.SemaphoreType.DMA((chips, CORES)),
        ],
        compiler_params=kernel_params(),
        name="pair_columns",
    )(chip.reshape(1), own_normed, arrived)


def factor_kernel(chip_ref, own_keys, other_keys, drift_ref, part0, part1, part2, part3, sum_ref):
    chips = own_keys.shape[0]
    total = jnp.zeros(sum_ref.shape, jnp.float32)
    for turn, part_ref in enumerate((part0, part1, part2, part3)):
        source = lax.rem(chip_ref[0] + (chips - turn), chips)
        for side, keys_ref in enumerate((own_keys, other_keys)):
            total = total + lax.dot_general(
                keys_ref[source],
                part_ref[side],
                (((0,), (0,)), ((), ())),
                preferred_element_type=jnp.float32,
            )
    sum_ref[...] = drift_ref[...] + inner_rate * total


def factor_columns(chip, own_keys, other_keys, drift_factor, parts):
    return pl.pallas_call(
        factor_kernel,
        out_shape=jax.ShapeDtypeStruct(drift_factor.shape, jnp.float32),
        in_specs=[pl.BlockSpec(memory_space=pltpu.SMEM)] + [whole_vmem()] * 7,
        out_specs=whole_vmem(),
        compiler_params=kernel_params(),
        name="factor_columns",
    )(chip.reshape(1), own_keys, other_keys, drift_factor, *parts)


def branch_kernel(hidden_ref, back_ref, gain_ref, pieces_ref, out, out_sem):
    tokens, width = hidden_ref.shape
    chips, _, span = back_ref.shape
    rows = 16
    count = pieces_ref.shape[1]
    each = rows // count
    columns = [(chip, column) for chip in range(chips) for column in range(0, span, 128)]

    def departure(place):
        run = pl.ds(place * each, each)
        return pltpu.make_async_copy(out.at[run], pieces_ref.at[run], out_sem)

    for place in range(tokens // rows):
        lines = pl.ds(place * rows, rows)

        def tile(chip, column, lines=lines):
            at = chip * span + column
            value = hidden_ref[lines, at : at + 128].astype(jnp.float32)
            back = back_ref[chip, lines, column : column + 128].astype(jnp.float32)
            return at, value, back * gain_ref[:, at : at + 128]

        squares = [jnp.zeros((rows, 128), jnp.float32)] * 2
        cross = [jnp.zeros((rows, 128), jnp.float32)] * 2
        for index, (chip, column) in enumerate(columns):
            _, value, scaled = tile(chip, column)
            squares[index % 2] = squares[index % 2] + value * value
            cross[index % 2] = cross[index % 2] + value * scaled
        total = jnp.sum(squares[0] + squares[1], -1, keepdims=True)
        recip = lax.rsqrt(total / width + 1e-05)
        mean = jnp.sum(cross[0] + cross[1], -1, keepdims=True) * recip / width
        share = recip * recip * mean
        for chip, column in columns:
            at, value, scaled = tile(chip, column)
            branch = (recip * scaled - share * value).astype(out.dtype)
            for part in range(each):
                lines_of = branch[part * count : (part + 1) * count]
                out[place * each + part, :, at : at + 128] = lines_of
        departure(place).start()
    pltpu.make_async_copy(out, pieces_ref, out_sem).wait()


def branch_pieces(hidden, back, gain_row, sections):
    tokens, width = hidden.shape
    shape = (sections, tokens // sections, width)
    return pl.pallas_call(
        branch_kernel,
        out_shape=pltpu.HBM(shape, jnp.bfloat16),
        in_specs=[whole_vmem()] * 3,
        out_specs=whole_hbm(),
        scratch_shapes=[pltpu.VMEM(shape, jnp.bfloat16), pltpu.SemaphoreType.DMA],
        compiler_params=kernel_params(),
        name="branch_pieces",
    )(pltpu.with_memory_space_constraint(hidden, pltpu.VMEM), back, gain_row)


def shards(hidden, norm_gain, key_grad, local_weight, drift, momentum, seeds):
    tokens, width = hidden.shape[2:]
    sections = lax.axis_size("section")
    islands = lax.axis_size("island")
    lanes = lax.axis_size("fsdp")
    chips = lanes // CORES
    lane = lax.axis_index("fsdp")
    chip, core = lane // CORES, lane - lane // CORES * CORES
    swap = [(i, i ^ 1) for i in range(lanes)]
    x_lines = [[c + CORES * i for i in range(chips)] for c in range(CORES)]
    gain_row = norm_gain
    own_hidden = hidden[0, 0]
    own_weight = local_weight[0, 0]
    slice_width = own_weight.shape[0]
    span = CORES * slice_width

    own_normed, swapped = prepare(core, own_hidden, gain_row, own_weight)
    swapped, sent_keys = lax.optimization_barrier((swapped, key_grad[0, 0]))
    arrived = lax.ppermute(swapped, "fsdp", swap)
    line_keys = lax.all_gather(sent_keys, "fsdp", axis_index_groups=x_lines)
    back = key_back_columns(core, line_keys, own_weight, arrived)
    back, own_normed, arrived = lax.optimization_barrier((back, own_normed, arrived))
    back = lax.all_to_all(back, "fsdp", 0, 0, axis_index_groups=x_lines)
    parts = list(pair_columns(chip, own_normed, arrived))
    basis_row = projection_basis(seeds[0], line_keys.shape[2], RANK)
    own_keys = lax.dot_general(
        line_keys,
        basis_row.astype(jnp.bfloat16),
        (((2,), (0,)), ((), ())),
        preferred_element_type=jnp.float32,
    ).astype(jnp.bfloat16)
    other_keys = lax.ppermute(own_keys, "fsdp", swap)
    back, own_keys, other_keys, *parts = lax.optimization_barrier(
        (back, own_keys, other_keys, *parts)
    )
    pieces = branch_pieces(own_hidden, back, gain_row, sections)

    pieces = lax.all_to_all(pieces, "section", 0, 0)

    for turn in (2, 1, 3):
        path = [(i, (i + CORES * turn) % lanes) for i in range(lanes)]
        parts[turn] = lax.ppermute(parts[turn], "fsdp", path)
    drift_factor = jnp.einsum("kr,dk->rd", basis_row, drift[0, 0], precision=lax.Precision.HIGH)
    factor = factor_columns(chip, own_keys, other_keys, drift_factor, parts)
    rank_share = momentum.shape[1]
    island = lax.axis_index("island")

    def rows_of(flip):
        at = jnp.bitwise_xor(island, flip) * rank_share
        return lax.dynamic_slice_in_dim(factor, at, rank_share, 0)

    def exchange(rows, flip):
        path = [(i, i ^ flip) for i in range(islands)]
        return lax.ppermute(rows.astype(jnp.bfloat16), "island", path).astype(jnp.float32)

    rows = exchange(jnp.concatenate([rows_of(1), rows_of(2)]), 1)
    own_sum = rows_of(0) + rows[:rank_share]
    other_sum = rows_of(3) + rows[rank_share:]
    sums, own_sum, other_sum, late_basis = lax.optimization_barrier(
        (suffix_sums(pieces), own_sum, other_sum, basis_row)
    )
    pieces = lax.all_to_all(sums, "section", 0, 0)
    input_grad = pieces.reshape(tokens, width)

    mean_weight = (1.0 + momentum_rate) / islands
    ride = momentum_rate * momentum_rate / mean_weight
    pair_sums = jnp.stack([own_sum + ride * momentum[0], other_sum]).astype(jnp.bfloat16)
    pair_sums = lax.all_gather(pair_sums, "island")
    other_pair = lax.dynamic_index_in_dim(pair_sums, jnp.bitwise_xor(island, 3), 0, False)[1]
    own_mean = (own_sum + other_pair.astype(jnp.float32)) / islands
    own_momentum = momentum_rate * momentum[0] + own_mean
    pair_sums = pair_sums.astype(jnp.float32)
    total = jnp.concatenate([pair_sums[i, 0] + pair_sums[i ^ 3, 1] for i in range(islands)])
    outer_update = (outer_rate * mean_weight) * jnp.einsum(
        "rd,kr->dk", total, late_basis, precision=lax.Precision.HIGH
    )
    return (input_grad[None, None], own_momentum[None], outer_update[None])


def solution(mesh):
    return jax.shard_map(
        shards,
        mesh=mesh,
        in_specs=(
            P("island", "section", "fsdp", None),
            P("section", None),
            P("island", "section", "fsdp", None),
            P("island", "section", "fsdp", None),
            P("island", "section", "fsdp", None),
            P("section", "island", "fsdp"),
            P("section"),
        ),
        out_specs=(
            P("island", "section", "fsdp", None),
            P("section", "island", "fsdp"),
            P("section", "fsdp", None),
        ),
        check_vma=False,
    )
```
